32 devices in a mesh: parts: 2 (over y), branch: 2 (over x), seq: 4 (over z), head: 2 (over core).
Axes of the slice: x: 2, y: 2, z: 4, core: 2. Of those that a mesh axis runs over, the one named last changes fastest.
Arguments:
- queries: bfloat16 [4, 48, 8, 128], P(('parts', 'branch'), 'seq', 'head'), parts along dimension 0, may hold values from -160 to 160
- output_cotangent: bfloat16 [4, 48, 8, 128], P(('parts', 'branch'), 'seq', 'head'), parts along dimension 0, may hold values from -6 to 6
- root_keys: bfloat16 [4096, 128], P(('parts', 'seq')), parts along dimension 0, may hold values from -8 to 8
- root_values: bfloat16 [4096, 128], P(('parts', 'seq')), parts along dimension 0, may hold values from -6 to 6
- branch_keys: bfloat16 [4, 2048, 128], P(('parts', 'branch'), 'seq'), parts along dimension 0, may hold values from -6 to 6
- branch_values: bfloat16 [4, 2048, 128], P(('parts', 'branch'), 'seq'), parts along dimension 0, may hold values from -6 to 6
- answer_positions: int32 [4, 48], P(('parts', 'branch')), parts along dimension 0, may hold values from 0 to 2047, as said below
Outputs:
- attention: bfloat16 [4, 48, 8, 128], P(('parts', 'branch'), 'seq', 'head'), parts along dimension 0
- query_gradient: float32 [4, 48, 8, 128], P(('parts', 'branch'), 'seq', 'head'), parts along dimension 0
- root_key_gradient: float32 [4096, 128], P(('parts', 'seq')), parts along dimension 0
- root_value_gradient: float32 [4096, 128], P(('parts', 'seq')), parts along dimension 0
- branch_key_gradient: float32 [4, 2048, 128], P(('parts', 'branch'), 'seq'), parts along dimension 0
- branch_value_gradient: float32 [4, 2048, 128], P(('parts', 'branch'), 'seq'), parts along dimension 0
The draws below stay inside these ranges and needn't reach their ends.
There are 2 independent parts, one for each index of `parts`. The reference program is written for one: setup_inputs(seed, part) draws one part's arguments, and reference() takes and returns one part's arrays. A program takes and returns all parts, laid end to end along the dimension named above; each array names one. Nothing has to cross between parts.
Inputs may be any that keep to these rules, and one draw needn't show every extreme that they name: `answer_positions`: within each branch the positions are strictly increasing.
All inputs are finite; a program needn't handle non-finite values.
Results may differ from the reference program's by a relative error of at most 0.015.
Values may be sent and summed in bfloat16 or wider, within the bound.
A program may use at most 64 MiB of HBM per device.

```python
import math
import jax
import jax.numpy as jnp
from jax import lax

HD = 128
HEADS = 8
NBR = 2
ROOT = 2048
BLEN = 2048
QA = 48


def shared_keys(key):
    return jax.random.normal(jax.random.fold_in(key, 11), (ROOT, HD), jnp.float32)


def draw_root_keys(key, part):
    return jnp.clip(shared_keys(key), -8.0, 8.0).astype(jnp.bfloat16)


def draw_queries(key, part):
    base = jax.random.normal(jax.random.fold_in(key, 23), (NBR, QA, HEADS, HD), jnp.float32)
    return jnp.clip(base, -160.0, 160.0).astype(jnp.bfloat16)


def draw_answer_positions(key, part):
    drawn = jax.random.randint(jax.random.fold_in(key, 43), (NBR, 1), BLEN // 4, BLEN + 1)
    first_branch = jnp.arange(NBR, dtype=jnp.int32)[:, None] == 0
    lengths = jnp.where(first_branch, BLEN, drawn).astype(jnp.int32)
    index = jnp.arange(QA, dtype=jnp.int32)[None, :]
    spacing = jnp.maximum(lengths // QA, 1)
    start = index * lengths // QA
    jitter = jax.random.randint(jax.random.fold_in(key, 47), (NBR, QA), 0, spacing)
    placed = start + jitter
    placed = jnp.where(index == QA - 1, lengths - 1, placed)
    return placed.astype(jnp.int32)


def block_levels(key, extent, shards, smallest, largest):
    loudness, own = 1.0, jax.random.fold_in(key, 6)
    for axis_at, shards_of in shards:
        heights = jnp.exp(jax.random.uniform(jax.random.fold_in(own, axis_at), (shards_of,), jnp.float32, smallest / len(shards), largest / len(shards)))
        loudness = loudness * jnp.repeat(heights, extent[axis_at] // shards_of).reshape([-1 if axis == axis_at else 1 for axis in range(len(extent))])
    return loudness


def gaussian(key, dims, scale, reach, split=(), kind=jnp.bfloat16):
    result = jax.random.normal(key, dims, jnp.float32) * scale
    if len(split) > 0:
        result = block_levels(key, dims, split, -0.22, 0.18) * result
    return jnp.clip(result, min=-reach, max=reach).astype(kind)


def setup_inputs(seed: int = 0, part: int = 0) -> dict:
    streams_of = jax.random.split(jax.random.key(seed), 8)
    own_keys = jax.random.split(jax.random.fold_in(streams_of[7], part), 8)
    return {
        "queries": draw_queries(jax.random.fold_in(jax.random.fold_in(streams_of[7], part), 71), part),
        "output_cotangent": gaussian(own_keys[1], (NBR, QA, HEADS, HD), 1.0, 6.0, ((0, 2), (1, 4), (2, 2))),
        "root_keys": draw_root_keys(jax.random.fold_in(jax.random.fold_in(streams_of[7], part), 71), part),
        "root_values": gaussian(own_keys[3], (ROOT, HD), 1.0, 6.0, ((0, 4),)),
        "branch_keys": gaussian(own_keys[4], (NBR, BLEN, HD), 1.0, 6.0, ((0, 2), (1, 4))),
        "branch_values": gaussian(own_keys[5], (NBR, BLEN, HD), 1.0, 6.0, ((0, 2), (1, 4))),
        "answer_positions": draw_answer_positions(jax.random.fold_in(jax.random.fold_in(streams_of[7], part), 71), part),
    }


NEG = -1e+30

def reference(queries, output_cotangent, root_keys, root_values, branch_keys, branch_values, answer_positions):
    score_scale = 1.0 / math.sqrt(HD)
    key_index = jnp.arange(ROOT + BLEN, dtype=jnp.int32)

    def one_branch(branch):
        all_keys = jnp.concatenate([root_keys, branch_keys[branch]], 0)
        all_values = jnp.concatenate([root_values, branch_values[branch]], 0)
        places = answer_positions[branch]
        visible = (key_index[None, :] < ROOT) | (key_index[None, :] - ROOT <= places[:, None])

        def one_head(running, head_index):
            query = queries[branch, :, head_index, :]
            cotangent = output_cotangent[branch, :, head_index, :]
            logits = jnp.dot(query, all_keys.T, preferred_element_type=jnp.float32) * score_scale
            logits = jnp.where(visible, logits, NEG)
            peak = lax.optimization_barrier(jnp.max(logits, axis=1))
            probs = jnp.exp(logits - peak[:, None])
            total = lax.optimization_barrier(jnp.sum(probs, axis=1))
            weighted = jnp.dot(probs.astype(jnp.bfloat16), all_values, preferred_element_type=jnp.float32)
            attended_exact = weighted / total[:, None]
            attended = attended_exact.astype(jnp.bfloat16)
            lse = peak + jnp.log(total)
            delta = lax.optimization_barrier(jnp.sum(cotangent.astype(jnp.float32) * attended_exact, axis=1))
            weights = jnp.exp(logits - lse[:, None])
            value_term = jnp.dot(weights.astype(jnp.bfloat16).T, cotangent, preferred_element_type=jnp.float32)
            product = jnp.dot(cotangent, all_values.T, preferred_element_type=jnp.float32)
            slope = (weights * (product - delta[:, None])).astype(jnp.bfloat16)
            query_term = jnp.dot(slope, all_keys, preferred_element_type=jnp.float32) * score_scale
            key_term = jnp.dot(slope.T, query, preferred_element_type=jnp.float32) * score_scale
            return ((running[0] + key_term, running[1] + value_term), (attended, query_term))
        start = (jnp.zeros((ROOT + BLEN, HD), jnp.float32), jnp.zeros((ROOT + BLEN, HD), jnp.float32))
        sums, stacked = lax.scan(one_head, start, jnp.arange(HEADS, dtype=jnp.int32))
        return (stacked[0], stacked[1], sums[0], sums[1])
    attended, query_terms, key_terms, value_terms = lax.map(one_branch, jnp.arange(NBR, dtype=jnp.int32))
    attention = jnp.transpose(attended, (0, 2, 1, 3))
    query_gradient = jnp.transpose(query_terms, (0, 2, 1, 3))
    root_key_gradient = lax.optimization_barrier(jnp.sum(key_terms[:, :ROOT], axis=0))
    root_value_gradient = lax.optimization_barrier(jnp.sum(value_terms[:, :ROOT], axis=0))
    return (attention, query_gradient, root_key_gradient, root_value_gradient, key_terms[:, ROOT:], value_terms[:, ROOT:])
```

```python
import functools
import math

import jax
import jax.numpy as jnp
from jax import lax
from jax.experimental import pallas as pl
from jax.experimental.pallas import tpu as pltpu
from jax.sharding import PartitionSpec as P

NEG = -1e30
ROWS = 256
F32 = jnp.float32
BF16 = jnp.bfloat16


def dot_last(left, right):
    return lax.dot_general(left, right, (((1,), (1,)), ((), ())), preferred_element_type=F32)


def dot_first(left, right):
    return lax.dot_general(left, right, (((0,), (0,)), ((), ())), preferred_element_type=F32)


def dot_plain(left, right):
    return jnp.dot(left, right, preferred_element_type=F32)


def remote(src, dst, send, recv, device):
    return pltpu.make_async_remote_copy(
        src_ref=src,
        dst_ref=dst,
        send_sem=send,
        recv_sem=recv,
        device_id=device,
        device_id_type=pl.DeviceIdType.MESH,
    )


def over(count, body):
    if count == 1:
        body(0)
    else:
        lax.fori_loop(0, count, lambda at, carry: (body(at), carry)[1], 0)


def kernel(
    sizes,
    q_ref, g_ref, pos_ref, rk_hbm, rv_hbm, bk_hbm, bv_hbm,
    att_out, dq_out, rk_out, rv_out, bk_out, bv_out,
    keys, values, rows_f32, qbuf, gbuf, stats, probs, product, weighted, place,
    att_send, att_recv, dq_acc, dq_send, dq_recv,
    root_part, root_recv, root_all, branch_all, slope_root, slope_branch, grads,
    load_sem, q_ss, q_rs, g_ss, g_rs, st_ss, st_rs, at_ss, at_rs, dq_ss, dq_rs,
    rs_ss, rs_rs, x_ss, x_rs, hd_ss, hd_rs, br_ss, br_rs,
):
    n, heads, branches = sizes
    me, my_head, my_branch = (
        lax.axis_index("seq"), lax.axis_index("head"), lax.axis_index("branch")
    )
    answers, per, width = q_ref.shape[1:]
    own = answers * per
    padded = qbuf.shape[0]
    chunks = padded // ROWS
    root_rows, branch_rows = rk_hbm.shape[0], bk_hbm.shape[1]
    piece = root_rows // heads
    scale = 1.0 / math.sqrt(width)

    def seq_to(d):
        return {"seq": lax.rem(me + d, n)}

    def seq_from(d):
        return lax.rem(me - d + n, n)

    def head_to(d):
        return {"head": lax.rem(my_head + d, heads)}

    def head_from(d):
        return lax.rem(my_head - d + heads, heads)

    def branch_to(d):
        return {"branch": lax.rem(my_branch + d, branches)}

    def branch_from(d):
        return lax.rem(my_branch - d + branches, branches)

    barrier = pltpu.get_barrier_semaphore()
    for to, count in ((seq_to, n), (head_to, heads), (branch_to, branches)):
        for d in range(1, count):
            pl.semaphore_signal(
                barrier, inc=1, device_id=to(d), device_id_type=pl.DeviceIdType.MESH
            )

    loads = [
        pltpu.make_async_copy(rk_hbm, keys.at[pl.ds(0, root_rows)], load_sem.at[0]),
        pltpu.make_async_copy(bk_hbm.at[0], keys.at[pl.ds(root_rows, branch_rows)], load_sem.at[1]),
        pltpu.make_async_copy(rv_hbm, values.at[pl.ds(0, root_rows)], load_sem.at[2]),
        pltpu.make_async_copy(bv_hbm.at[0], values.at[pl.ds(root_rows, branch_rows)], load_sem.at[3]),
    ]
    for load in loads:
        load.start()

    mine = pl.ds(pl.multiple_of(me * own, 16), own)
    for at, (source, target) in enumerate(((q_ref, qbuf), (g_ref, gbuf))):
        for i in range(answers):
            rows_f32[at, i * per:(i + 1) * per, :] = source[0, i].astype(F32)
        target[mine, :] = rows_f32[at].astype(BF16)
        if padded > n * own:
            target[n * own:, :] = jnp.zeros((padded - n * own, width), BF16)

    pl.semaphore_wait(barrier, (n - 1) + (heads - 1) + (branches - 1))

    sends = []

    def send(*pieces):
        copy = remote(*pieces)
        copy.start()
        sends.append(copy)

    for buf, ss, rs in ((qbuf, q_ss, q_rs), (gbuf, g_ss, g_rs)):
        for d in range(1, n):
            send(buf.at[mine], buf.at[mine], ss.at[d - 1], rs.at[d - 1], seq_to(d))

    def arrived_rows(buf, ss, rs):
        for d in range(1, n):
            rows = pl.ds(pl.multiple_of(seq_from(d) * own, 16), own)
            remote(buf.at[rows], buf.at[rows], ss.at[d - 1], rs.at[d - 1], seq_to(d)).wait_recv()

    total = pos_ref.shape[1]
    spot = jnp.broadcast_to(pos_ref[...], (8, total))
    high = (spot >> 7).astype(F32).astype(BF16)
    low = (spot & 127).astype(F32).astype(BF16)

    def expand(c):
        row = lax.broadcasted_iota(jnp.int32, (total, ROWS), 1) + c * ROWS
        answer = lax.broadcasted_iota(jnp.int32, (total, ROWS), 0)
        pick = (row >= answer * per) & (row < answer * per + per)
        pick = jnp.where(pick, 1.0, 0.0).astype(BF16)
        place[c] = dot_plain(high, pick) * 128.0 + dot_plain(low, pick)

    over(chunks, expand)

    for load in loads:
        load.wait()
    arrived_rows(qbuf, q_ss, q_rs)

    key_place = (
        lax.broadcasted_iota(jnp.int32, (branch_rows, ROWS), 0) + me * branch_rows
    ).astype(F32)

    def rows_of(c):
        return pl.ds(c * ROWS if isinstance(c, int) else pl.multiple_of(c * ROWS, ROWS), ROWS)

    def scores(c):
        q = qbuf[rows_of(c), :]
        on_root = dot_last(keys[:root_rows, :], q) * scale
        on_branch = dot_last(keys[root_rows:, :], q) * scale
        on_branch = jnp.where(key_place <= place[c, 0:1, :], on_branch, NEG)
        peak = jnp.maximum(
            jnp.max(on_root, axis=0, keepdims=True), jnp.max(on_branch, axis=0, keepdims=True)
        )
        p_root = jnp.exp(on_root - peak)
        p_branch = jnp.exp(on_branch - peak)
        probs[c, :root_rows, :] = p_root
        probs[c, root_rows:, :] = p_branch
        sums = jnp.sum(p_root, axis=0, keepdims=True) + jnp.sum(p_branch, axis=0, keepdims=True)
        share = dot_first(values[:root_rows, :], p_root.astype(BF16))
        share = share + dot_first(values[root_rows:, :], p_branch.astype(BF16))
        weighted[c] = share
        stats[me, c, 0:1, :] = peak
        stats[me, c, 1:2, :] = sums

    over(chunks, scores)
    arrived_rows(gbuf, g_ss, g_rs)

    def dots(c):
        turned = gbuf[rows_of(c), :].astype(F32).T
        stats[me, c, 2:3, :] = jnp.sum(weighted[c] * turned, axis=0, keepdims=True)
        stats[me, c, 3:8, :] = jnp.zeros((5, ROWS), F32)

    over(chunks, dots)
    for d in range(1, n):
        send(stats.at[me], stats.at[me], st_ss.at[d - 1], st_rs.at[d - 1], seq_to(d))

    def products(c):
        g = gbuf[rows_of(c), :]
        product[c, :root_rows, :] = dot_last(values[:root_rows, :], g)
        product[c, root_rows:, :] = dot_last(values[root_rows:, :], g)

    over(chunks, products)
    for d in range(1, n):
        at = seq_from(d)
        remote(stats.at[at], stats.at[at], st_ss.at[d - 1], st_rs.at[d - 1], seq_to(d)).wait_recv()

    def combine(c):
        peak = stats[0, c, 0:1, :]
        for s in range(1, n):
            peak = jnp.maximum(peak, stats[s, c, 0:1, :])
        sums, dotted = jnp.zeros((1, ROWS), F32), jnp.zeros((1, ROWS), F32)
        for s in range(n):
            factor = jnp.exp(stats[s, c, 0:1, :] - peak)
            sums = sums + stats[s, c, 1:2, :] * factor
            dotted = dotted + stats[s, c, 2:3, :] * factor
        factor = jnp.exp(stats[me, c, 0:1, :] - peak) / sums
        place[c, 1:2, :] = factor
        place[c, 2:3, :] = dotted / sums

    over(chunks, combine)

    def backward(c, start, count, slope):
        rows = rows_of(c)
        weights = probs[c, start:start + count, :] * place[c, 1:2, :]
        value_term = dot_plain(weights.astype(BF16), gbuf[rows, :])
        gap = product[c, start:start + count, :] - place[c, 2:3, :]
        sloped = (weights * gap).astype(BF16)
        slope[c] = sloped
        key_term = dot_plain(sloped, qbuf[rows, :]) * scale
        return value_term, key_term

    def sweep(start, count, slope):
        if chunks == 1:
            return backward(0, start, count, slope)
        grads[0, :count, :] = jnp.zeros((count, width), F32)
        grads[1, :count, :] = jnp.zeros((count, width), F32)

        def add(c):
            value_term, key_term = backward(c, start, count, slope)
            grads[0, :count, :] += value_term
            grads[1, :count, :] += key_term

        over(chunks, add)
        return grads[0, :count, :], grads[1, :count, :]

    for at, term in enumerate(sweep(0, root_rows, slope_root)):
        root_part[at] = term.astype(BF16)
        for d in range(1, heads):
            far = pl.ds(pl.multiple_of(lax.rem(my_head + d, heads) * piece, 16), piece)
            send(
                root_part.at[at, far], root_recv.at[at, d - 1],
                rs_ss.at[at, d - 1], rs_rs.at[at, d - 1], head_to(d),
            )

    near = pl.ds(pl.multiple_of(my_head * piece, 16), piece)
    for at in range(2):
        term = root_part[at, near, :].astype(F32)
        for d in range(1, heads):
            remote(
                root_recv.at[at, d - 1], root_recv.at[at, d - 1],
                rs_ss.at[at, d - 1], rs_rs.at[at, d - 1], head_to(d),
            ).wait_recv()
            term = term + root_recv[at, d - 1].astype(F32)
        root_all[at, my_branch, my_head] = term.astype(BF16)
        block = root_all.at[at, my_branch, my_head]
        for d in range(1, branches):
            send(block, block, x_ss.at[at, d - 1], x_rs.at[at, d - 1], branch_to(d))
        for d in range(1, heads):
            send(block, block, hd_ss.at[at, 0, d - 1], hd_rs.at[at, 0, d - 1], head_to(d))

    for at, term in enumerate(sweep(root_rows, branch_rows, slope_branch)):
        branch_all[at, my_head] = term.astype(BF16)
        block = branch_all.at[at, my_head]
        for d in range(1, heads):
            send(block, block, br_ss.at[at, d - 1], br_rs.at[at, d - 1], head_to(d))

    def query_terms(c):
        term = dot_first(slope_root[c], keys[:root_rows, :])
        term = term + dot_first(slope_branch[c], keys[root_rows:, :])
        dq_send[rows_of(c), :] = (term * scale).astype(BF16)
        att_send[rows_of(c), :] = (weighted[c] * place[c, 1:2, :]).T.astype(BF16)

    over(chunks, query_terms)
    for buf, into, ss, rs in ((dq_send, dq_recv, dq_ss, dq_rs), (att_send, att_recv, at_ss, at_rs)):
        for d in range(1, n):
            far = pl.ds(pl.multiple_of(lax.rem(me + d, n) * own, 16), own)
            send(buf.at[far], into.at[d - 1], ss.at[d - 1], rs.at[d - 1], seq_to(d))

    for at in range(2):
        for d in range(1, branches):
            block = root_all.at[at, branch_from(d), my_head]
            remote(block, block, x_ss.at[at, d - 1], x_rs.at[at, d - 1], branch_to(d)).wait_recv()
            for e in range(1, heads):
                send(block, block, hd_ss.at[at, d, e - 1], hd_rs.at[at, d, e - 1], head_to(e))

    for at, out in ((0, bv_out), (1, bk_out)):
        for d in range(1, heads):
            block = branch_all.at[at, head_from(d)]
            remote(block, block, br_ss.at[at, d - 1], br_rs.at[at, d - 1], head_to(d)).wait_recv()
        term = branch_all[at, 0].astype(F32)
        for h in range(1, heads):
            term = term + branch_all[at, h].astype(F32)
        out[0] = term

    for at, (buf, into, ss, rs, out) in enumerate((
        (dq_send, dq_recv, dq_ss, dq_rs, dq_out), (att_send, att_recv, at_ss, at_rs, att_out)
    )):
        term = buf[mine, :].astype(F32)
        for d in range(1, n):
            remote(
                into.at[d - 1], into.at[d - 1], ss.at[d - 1], rs.at[d - 1], seq_to(d)
            ).wait_recv()
            term = term + into[d - 1].astype(F32)
        rows_f32[at] = term
        for i in range(answers):
            out[0, i] = rows_f32[at, i * per:(i + 1) * per, :].astype(out.dtype)

    for at, out in ((0, rv_out), (1, rk_out)):
        for b in range(branches):
            for d in range(1, heads):
                block = root_all.at[at, lax.rem(my_branch - b + branches, branches), head_from(d)]
                remote(
                    block, block, hd_ss.at[at, b, d - 1], hd_rs.at[at, b, d - 1], head_to(d)
                ).wait_recv()
        for h in range(heads):
            term = root_all[at, 0, h].astype(F32)
            for b in range(1, branches):
                term = term + root_all[at, b, h].astype(F32)
            out[h * piece:(h + 1) * piece, :] = term

    for copy in sends:
        copy.wait_send()


def per_device(sizes, queries, output_cotangent, root_keys, root_values, branch_keys,
               branch_values, answer_positions):
    n, heads, branches = sizes
    answers, per, width = queries.shape[1:]
    own = answers * per
    padded = -(-n * own // ROWS) * ROWS
    chunks = padded // ROWS
    root_rows, branch_rows = root_keys.shape[0], branch_keys.shape[1]
    key_rows = root_rows + branch_rows
    piece = root_rows // heads
    vmem = pl.BlockSpec(memory_space=pltpu.VMEM)
    whole = pl.BlockSpec(memory_space=pl.ANY)

    def sem(*shape):
        return pltpu.SemaphoreType.DMA(tuple(max(1, size) for size in shape))

    z, h, b = max(1, n - 1), max(1, heads - 1), max(1, branches - 1)
    scratch = [
        pltpu.VMEM((key_rows, width), BF16),
        pltpu.VMEM((key_rows, width), BF16),
        pltpu.VMEM((2, own, width), F32),
        pltpu.VMEM((padded, width), BF16),
        pltpu.VMEM((padded, width), BF16),
        pltpu.VMEM((n, chunks, 8, ROWS), F32),
        pltpu.VMEM((chunks, key_rows, ROWS), F32),
        pltpu.VMEM((chunks, key_rows, ROWS), F32),
        pltpu.VMEM((chunks, width, ROWS), F32),
        pltpu.VMEM((chunks, 8, ROWS), F32),
        pltpu.VMEM((padded, width), BF16),
        pltpu.VMEM((z, own, width), BF16),
        pltpu.VMEM((8, 128), F32),
        pltpu.VMEM((padded, width), BF16),
        pltpu.VMEM((z, own, width), BF16),
        pltpu.VMEM((2, root_rows, width), BF16),
        pltpu.VMEM((2, h, piece, width), BF16),
        pltpu.VMEM((2, branches, heads, piece, width), BF16),
        pltpu.VMEM((2, heads, branch_rows, width), BF16),
        pltpu.VMEM((chunks, root_rows, ROWS), BF16),
        pltpu.VMEM((chunks, branch_rows, ROWS), BF16),
        pltpu.VMEM((2, max(root_rows, branch_rows), width), F32),
        sem(4),
        sem(z), sem(z), sem(z), sem(z), sem(z), sem(z), sem(z), sem(z), sem(z), sem(z),
        sem(2, h), sem(2, h), sem(2, b), sem(2, b),
        sem(2, branches, h), sem(2, branches, h), sem(2, h), sem(2, h),
    ]
    outs = (
        jax.ShapeDtypeStruct(queries.shape, BF16),
        jax.ShapeDtypeStruct(queries.shape, F32),
        jax.ShapeDtypeStruct(root_keys.shape, F32),
        jax.ShapeDtypeStruct(root_values.shape, F32),
        jax.ShapeDtypeStruct(branch_keys.shape, F32),
        jax.ShapeDtypeStruct(branch_values.shape, F32),
    )
    return pl.pallas_call(
        functools.partial(kernel, sizes),
        out_shape=outs,
        in_specs=[vmem, vmem, vmem, whole, whole, whole, whole],
        out_specs=[vmem] * 6,
        scratch_shapes=scratch,
        compiler_params=pltpu.CompilerParams(
            collective_id=0, has_side_effects=True, vmem_limit_bytes=48 * 1024 * 1024
        ),
    )(queries, output_cotangent, answer_positions, root_keys, root_values, branch_keys, branch_values)


def solution(mesh):
    sizes = (mesh.shape["seq"], mesh.shape["head"], mesh.shape["branch"])
    rows = P(("parts", "branch"), "seq", "head", None)
    root = P(("parts", "seq"), None)
    branch = P(("parts", "branch"), "seq", None)
    return jax.shard_map(
        functools.partial(per_device, sizes),
        mesh=mesh,
        in_specs=(rows, rows, root, root, branch, branch, P(("parts", "branch"), None)),
        out_specs=(rows, rows, root, root, branch, branch),
        check_vma=False,
    )
```

```python
import functools
import math

import jax
import jax.numpy as jnp
from jax import lax
from jax.experimental import pallas as pl
from jax.experimental.pallas import tpu as pltpu
from jax.sharding import PartitionSpec as P

NEG = -1e30
ROWS = 256
F32 = jnp.float32
BF16 = jnp.bfloat16


def dot_last(left, right):
    return lax.dot_general(left, right, (((1,), (1,)), ((), ())), preferred_element_type=F32)


def dot_first(left, right):
    return lax.dot_general(left, right, (((0,), (0,)), ((), ())), preferred_element_type=F32)


def dot_plain(left, right):
    return jnp.dot(left, right, preferred_element_type=F32)


def remote(src, dst, send, recv, device):
    return pltpu.make_async_remote_copy(
        src_ref=src,
        dst_ref=dst,
        send_sem=send,
        recv_sem=recv,
        device_id=device,
        device_id_type=pl.DeviceIdType.MESH,
    )


def over(count, body):
    if count == 1:
        body(0)
    else:
        lax.fori_loop(0, count, lambda at, carry: (body(at), carry)[1], 0)


def kernel(
    sizes,
    q_hbm, g_hbm, pos_hbm, rk_hbm, rv_hbm, bk_hbm, bv_hbm,
    att_out, dq_out, rk_out, rv_out, bk_out, bv_out,
    rows_in, pos_ref, keys, values, rows_f32, qbuf, gbuf, stats, probs, product, weighted, place,
    att_send, att_recv, dq_acc, dq_send, dq_recv,
    root_part, root_recv, root_all, branch_all, slope_root, slope_branch, grads,
    load_sem, q_ss, q_rs, g_ss, g_rs, st_ss, st_rs, at_ss, at_rs, dq_ss, dq_rs,
    rs_ss, rs_rs, x_ss, x_rs, hd_ss, hd_rs, br_ss, br_rs,
):
    n, heads, branches = sizes
    me, my_head, my_branch = (
        lax.axis_index("seq"), lax.axis_index("head"), lax.axis_index("branch")
    )
    answers, per, width = q_hbm.shape[1:]
    own = answers * per
    padded = qbuf.shape[0]
    chunks = padded // ROWS
    root_rows, branch_rows = rk_hbm.shape[0], bk_hbm.shape[1]
    piece = root_rows // heads
    scale = 1.0 / math.sqrt(width)

    def seq_to(d):
        return {"seq": lax.rem(me + d, n)}

    def seq_from(d):
        return lax.rem(me - d + n, n)

    def head_to(d):
        return {"head": lax.rem(my_head + d, heads)}

    def head_from(d):
        return lax.rem(my_head - d + heads, heads)

    def branch_to(d):
        return {"branch": lax.rem(my_branch + d, branches)}

    def branch_from(d):
        return lax.rem(my_branch - d + branches, branches)

    barrier = pltpu.get_barrier_semaphore()
    for to, count in ((seq_to, n), (head_to, heads), (branch_to, branches)):
        for d in range(1, count):
            pl.semaphore_signal(
                barrier, inc=1, device_id=to(d), device_id_type=pl.DeviceIdType.MESH
            )

    loads = [
        pltpu.make_async_copy(q_hbm.at[0], rows_in.at[0], load_sem.at[4]),
        pltpu.make_async_copy(g_hbm.at[0], rows_in.at[1], load_sem.at[5]),
        pltpu.make_async_copy(pos_hbm, pos_ref, load_sem.at[6]),
        pltpu.make_async_copy(rk_hbm, keys.at[pl.ds(0, root_rows)], load_sem.at[0]),
        pltpu.make_async_copy(bk_hbm.at[0], keys.at[pl.ds(root_rows, branch_rows)], load_sem.at[1]),
        pltpu.make_async_copy(rv_hbm, values.at[pl.ds(0, root_rows)], load_sem.at[2]),
        pltpu.make_async_copy(bv_hbm.at[0], values.at[pl.ds(root_rows, branch_rows)], load_sem.at[3]),
    ]
    for load in loads:
        load.start()

    mine = pl.ds(pl.multiple_of(me * own, 16), own)
    for at, target in enumerate((qbuf, gbuf)):
        loads[at].wait()
        for i in range(answers):
            rows_f32[at, i * per:(i + 1) * per, :] = rows_in[at, i].astype(F32)
        target[mine, :] = rows_f32[at].astype(BF16)
        if padded > n * own:
            target[n * own:, :] = jnp.zeros((padded - n * own, width), BF16)

    pl.semaphore_wait(barrier, (n - 1) + (heads - 1) + (branches - 1))

    sends = []

    def send(*pieces):
        copy = remote(*pieces)
        copy.start()
        sends.append(copy)

    for buf, ss, rs in ((qbuf, q_ss, q_rs), (gbuf, g_ss, g_rs)):
        for d in range(1, n):
            send(buf.at[mine], buf.at[mine], ss.at[d - 1], rs.at[d - 1], seq_to(d))

    def arrived_rows(buf, ss, rs):
        for d in range(1, n):
            rows = pl.ds(pl.multiple_of(seq_from(d) * own, 16), own)
            remote(buf.at[rows], buf.at[rows], ss.at[d - 1], rs.at[d - 1], seq_to(d)).wait_recv()

    loads[2].wait()
    total = pos_ref.shape[1]
    spot = jnp.broadcast_to(pos_ref[...], (8, total))
    high = (spot >> 7).astype(F32).astype(BF16)
    low = (spot & 127).astype(F32).astype(BF16)

    def expand(c):
        row = lax.broadcasted_iota(jnp.int32, (total, ROWS), 1) + c * ROWS
        answer = lax.broadcasted_iota(jnp.int32, (total, ROWS), 0)
        pick = (row >= answer * per) & (row < answer * per + per)
        pick = jnp.where(pick, 1.0, 0.0).astype(BF16)
        place[c] = dot_plain(high, pick) * 128.0 + dot_plain(low, pick)

    over(chunks, expand)

    for load in loads[3:]:
        load.wait()
    arrived_rows(qbuf, q_ss, q_rs)

    key_place = (
        lax.broadcasted_iota(jnp.int32, (branch_rows, ROWS), 0) + me * branch_rows
    ).astype(F32)

    def rows_of(c):
        return pl.ds(c * ROWS if isinstance(c, int) else pl.multiple_of(c * ROWS, ROWS), ROWS)

    def scores(c):
        q = qbuf[rows_of(c), :]
        on_root = dot_last(keys[:root_rows, :], q) * scale
        on_branch = dot_last(keys[root_rows:, :], q) * scale
        on_branch = jnp.where(key_place <= place[c, 0:1, :], on_branch, NEG)
        peak = jnp.maximum(
            jnp.max(on_root, axis=0, keepdims=True), jnp.max(on_branch, axis=0, keepdims=True)
        )
        p_root = jnp.exp(on_root - peak)
        p_branch = jnp.exp(on_branch - peak)
        probs[c, :root_rows, :] = p_root
        probs[c, root_rows:, :] = p_branch
        sums = jnp.sum(p_root, axis=0, keepdims=True) + jnp.sum(p_branch, axis=0, keepdims=True)
        share = dot_first(values[:root_rows, :], p_root.astype(BF16))
        share = share + dot_first(values[root_rows:, :], p_branch.astype(BF16))
        weighted[c] = share
        stats[me, c, 0:1, :] = peak
        stats[me, c, 1:2, :] = sums

    over(chunks, scores)
    arrived_rows(gbuf, g_ss, g_rs)

    def dots(c):
        turned = gbuf[rows_of(c), :].astype(F32).T
        stats[me, c, 2:3, :] = jnp.sum(weighted[c] * turned, axis=0, keepdims=True)
        stats[me, c, 3:8, :] = jnp.zeros((5, ROWS), F32)

    over(chunks, dots)
    for d in range(1, n):
        send(stats.at[me], stats.at[me], st_ss.at[d - 1], st_rs.at[d - 1], seq_to(d))

    def products(c):
        g = gbuf[rows_of(c), :]
        product[c, :root_rows, :] = dot_last(values[:root_rows, :], g)
        product[c, root_rows:, :] = dot_last(values[root_rows:, :], g)

    over(chunks, products)
    for d in range(1, n):
        at = seq_from(d)
        remote(stats.at[at], stats.at[at], st_ss.at[d - 1], st_rs.at[d - 1], seq_to(d)).wait_recv()

    def combine(c):
        peak = stats[0, c, 0:1, :]
        for s in range(1, n):
            peak = jnp.maximum(peak, stats[s, c, 0:1, :])
        sums, dotted = jnp.zeros((1, ROWS), F32), jnp.zeros((1, ROWS), F32)
        for s in range(n):
            factor = jnp.exp(stats[s, c, 0:1, :] - peak)
            sums = sums + stats[s, c, 1:2, :] * factor
            dotted = dotted + stats[s, c, 2:3, :] * factor
        factor = jnp.exp(stats[me, c, 0:1, :] - peak) / sums
        place[c, 1:2, :] = factor
        place[c, 2:3, :] = dotted / sums

    over(chunks, combine)

    def value_term(c, start, count, slope):
        weights = probs[c, start:start + count, :] * place[c, 1:2, :]
        return dot_plain(weights.astype(BF16), gbuf[rows_of(c), :])

    def key_term(c, start, count, slope):
        weights = probs[c, start:start + count, :] * place[c, 1:2, :]
        gap = product[c, start:start + count, :] - place[c, 2:3, :]
        sloped = (weights * gap).astype(BF16)
        slope[c] = sloped
        return dot_plain(sloped, qbuf[rows_of(c), :]) * scale

    def sweep(term, start, count, slope):
        if chunks == 1:
            return term(0, start, count, slope)
        grads[:count, :] = jnp.zeros((count, width), F32)

        def add(c):
            grads[:count, :] += term(c, start, count, slope)

        over(chunks, add)
        return grads[:count, :]

    for at, term in enumerate((value_term, key_term)):
        root_part[at] = sweep(term, 0, root_rows, slope_root).astype(BF16)
        for d in range(1, heads):
            far = pl.ds(pl.multiple_of(lax.rem(my_head + d, heads) * piece, 16), piece)
            send(
                root_part.at[at, far], root_recv.at[at, d - 1],
                rs_ss.at[at, d - 1], rs_rs.at[at, d - 1], head_to(d),
            )

    near = pl.ds(pl.multiple_of(my_head * piece, 16), piece)
    for at in range(2):
        term = root_part[at, near, :].astype(F32)
        for d in range(1, heads):
            remote(
                root_recv.at[at, d - 1], root_recv.at[at, d - 1],
                rs_ss.at[at, d - 1], rs_rs.at[at, d - 1], head_to(d),
            ).wait_recv()
            term = term + root_recv[at, d - 1].astype(F32)
        root_all[at, my_branch, my_head] = term.astype(BF16)
        block = root_all.at[at, my_branch, my_head]
        for d in range(1, branches):
            send(block, block, x_ss.at[at, d - 1], x_rs.at[at, d - 1], branch_to(d))
        for d in range(1, heads):
            send(block, block, hd_ss.at[at, 0, d - 1], hd_rs.at[at, 0, d - 1], head_to(d))

    for at, term in enumerate((value_term, key_term)):
        branch_all[at, my_head] = sweep(term, root_rows, branch_rows, slope_branch).astype(BF16)
        block = branch_all.at[at, my_head]
        for d in range(1, heads):
            send(block, block, br_ss.at[at, d - 1], br_rs.at[at, d - 1], head_to(d))

    def query_terms(c):
        term = dot_first(slope_root[c], keys[:root_rows, :])
        term = term + dot_first(slope_branch[c], keys[root_rows:, :])
        dq_send[rows_of(c), :] = (term * scale).astype(BF16)
        att_send[rows_of(c), :] = (weighted[c] * place[c, 1:2, :]).T.astype(BF16)

    over(chunks, query_terms)
    for buf, into, ss, rs in ((dq_send, dq_recv, dq_ss, dq_rs), (att_send, att_recv, at_ss, at_rs)):
        for d in range(1, n):
            far = pl.ds(pl.multiple_of(lax.rem(me + d, n) * own, 16), own)
            send(buf.at[far], into.at[d - 1], ss.at[d - 1], rs.at[d - 1], seq_to(d))

    for at in range(2):
        for d in range(1, branches):
            block = root_all.at[at, branch_from(d), my_head]
            remote(block, block, x_ss.at[at, d - 1], x_rs.at[at, d - 1], branch_to(d)).wait_recv()
            for e in range(1, heads):
                send(block, block, hd_ss.at[at, d, e - 1], hd_rs.at[at, d, e - 1], head_to(e))

    for at, out in ((0, bv_out), (1, bk_out)):
        for d in range(1, heads):
            block = branch_all.at[at, head_from(d)]
            remote(block, block, br_ss.at[at, d - 1], br_rs.at[at, d - 1], head_to(d)).wait_recv()
        term = branch_all[at, 0].astype(F32)
        for h in range(1, heads):
            term = term + branch_all[at, h].astype(F32)
        out[0] = term

    for at, (buf, into, ss, rs, out) in enumerate((
        (dq_send, dq_recv, dq_ss, dq_rs, dq_out), (att_send, att_recv, at_ss, at_rs, att_out)
    )):
        term = buf[mine, :].astype(F32)
        for d in range(1, n):
            remote(
                into.at[d - 1], into.at[d - 1], ss.at[d - 1], rs.at[d - 1], seq_to(d)
            ).wait_recv()
            term = term + into[d - 1].astype(F32)
        rows_f32[at] = term
        for i in range(answers):
            out[0, i] = rows_f32[at, i * per:(i + 1) * per, :].astype(out.dtype)

    for at, out in ((0, rv_out), (1, rk_out)):
        for b in range(branches):
            for d in range(1, heads):
                block = root_all.at[at, lax.rem(my_branch - b + branches, branches), head_from(d)]
                remote(
                    block, block, hd_ss.at[at, b, d - 1], hd_rs.at[at, b, d - 1], head_to(d)
                ).wait_recv()
        for h in range(heads):
            term = root_all[at, 0, h].astype(F32)
            for b in range(1, branches):
                term = term + root_all[at, b, h].astype(F32)
            out[h * piece:(h + 1) * piece, :] = term

    for copy in sends:
        copy.wait_send()


def hand_out(*refs):
    sems = refs[12]
    copies = [pltpu.make_async_copy(refs[i], refs[6 + i], sems.at[i]) for i in range(6)]
    for copy in copies:
        copy.start()
    for copy in copies:
        copy.wait()


def per_device(sizes, queries, output_cotangent, root_keys, root_values, branch_keys,
               branch_values, answer_positions):
    n, heads, branches = sizes
    answers, per, width = queries.shape[1:]
    own = answers * per
    padded = -(-n * own // ROWS) * ROWS
    chunks = padded // ROWS
    root_rows, branch_rows = root_keys.shape[0], branch_keys.shape[1]
    key_rows = root_rows + branch_rows
    piece = root_rows // heads
    vmem = pl.BlockSpec(memory_space=pltpu.VMEM)
    whole = pl.BlockSpec(memory_space=pltpu.HBM)

    def sem(*shape):
        return pltpu.SemaphoreType.DMA(tuple(max(1, size) for size in shape))

    z, h, b = max(1, n - 1), max(1, heads - 1), max(1, branches - 1)
    scratch = [
        pltpu.VMEM((2, answers, per, width), BF16),
        pltpu.VMEM(answer_positions.shape, jnp.int32),
        pltpu.VMEM((key_rows, width), BF16),
        pltpu.VMEM((key_rows, width), BF16),
        pltpu.VMEM((2, own, width), F32),
        pltpu.VMEM((padded, width), BF16),
        pltpu.VMEM((padded, width), BF16),
        pltpu.VMEM((n, chunks, 8, ROWS), F32),
        pltpu.VMEM((chunks, key_rows, ROWS), F32),
        pltpu.VMEM((chunks, key_rows, ROWS), F32),
        pltpu.VMEM((chunks, width, ROWS), F32),
        pltpu.VMEM((chunks, 8, ROWS), F32),
        pltpu.VMEM((padded, width), BF16),
        pltpu.VMEM((z, own, width), BF16),
        pltpu.VMEM((8, 128), F32),
        pltpu.VMEM((padded, width), BF16),
        pltpu.VMEM((z, own, width), BF16),
        pltpu.VMEM((2, root_rows, width), BF16),
        pltpu.VMEM((2, h, piece, width), BF16),
        pltpu.VMEM((2, branches, heads, piece, width), BF16),
        pltpu.VMEM((2, heads, branch_rows, width), BF16),
        pltpu.VMEM((chunks, root_rows, ROWS), BF16),
        pltpu.VMEM((chunks, branch_rows, ROWS), BF16),
        pltpu.VMEM((max(root_rows, branch_rows), width), F32),
        sem(7),
        sem(z), sem(z), sem(z), sem(z), sem(z), sem(z), sem(z), sem(z), sem(z), sem(z),
        sem(2, h), sem(2, h), sem(2, b), sem(2, b),
        sem(2, branches, h), sem(2, branches, h), sem(2, h), sem(2, h),
    ]
    outs = (
        jax.ShapeDtypeStruct(queries.shape, BF16),
        jax.ShapeDtypeStruct(queries.shape, F32),
        jax.ShapeDtypeStruct(root_keys.shape, F32),
        jax.ShapeDtypeStruct(root_values.shape, F32),
        jax.ShapeDtypeStruct(branch_keys.shape, F32),
        jax.ShapeDtypeStruct(branch_values.shape, F32),
    )
    results = pl.pallas_call(
        functools.partial(kernel, sizes),
        out_shape=outs,
        in_specs=[whole] * 7,
        out_specs=[vmem] * 6,
        scratch_shapes=scratch,
        compiler_params=pltpu.CompilerParams(
            collective_id=0, has_side_effects=True, vmem_limit_bytes=48 * 1024 * 1024
        ),
    )(*(
        pltpu.with_memory_space_constraint(array, pltpu.HBM) for array in (
            queries, output_cotangent, answer_positions, root_keys, root_values,
            branch_keys, branch_values,
        )
    ))
    return pl.pallas_call(
        hand_out,
        out_shape=outs,
        in_specs=[vmem] * 6,
        out_specs=[whole] * 6,
        scratch_shapes=[pltpu.SemaphoreType.DMA((6,))],
    )(*results)


def solution(mesh):
    sizes = (mesh.shape["seq"], mesh.shape["head"], mesh.shape["branch"])
    rows = P(("parts", "branch"), "seq", "head", None)
    root = P(("parts", "seq"), None)
    branch = P(("parts", "branch"), "seq", None)
    return jax.shard_map(
        functools.partial(per_device, sizes),
        mesh=mesh,
        in_specs=(rows, rows, root, root, branch, branch, P(("parts", "branch"), None)),
        out_specs=(rows, rows, root, root, branch, branch),
        check_vma=False,
    )
```

```python
import functools
import math

import jax
import jax.numpy as jnp
from jax import lax
from jax.experimental import pallas as pl
from jax.experimental.pallas import tpu as pltpu
from jax.sharding import PartitionSpec as P

NEG = -1e30
ROWS = 256
F32 = jnp.float32
BF16 = jnp.bfloat16


def dot_last(left, right):
    return lax.dot_general(left, right, (((1,), (1,)), ((), ())), preferred_element_type=F32)


def dot_first(left, right):
    return lax.dot_general(left, right, (((0,), (0,)), ((), ())), preferred_element_type=F32)


def dot_plain(left, right):
    return jnp.dot(left, right, preferred_element_type=F32)


def remote(src, dst, send, recv, device):
    return pltpu.make_async_remote_copy(
        src_ref=src,
        dst_ref=dst,
        send_sem=send,
        recv_sem=recv,
        device_id=device,
        device_id_type=pl.DeviceIdType.MESH,
    )


def over(count, body):
    if count == 1:
        body(0)
    else:
        lax.fori_loop(0, count, lambda at, carry: (body(at), carry)[1], 0)


def kernel(
    sizes,
    q_hbm, g_hbm, pos_hbm, rk_hbm, rv_hbm, bk_hbm, bv_hbm,
    att_out, dq_out, rk_out, rv_out, bk_out, bv_out,
    pos_ref, keys, values, rows_f32, qbuf, gbuf, stats, probs, product, weighted, place,
    att_send, att_recv, dq_acc, dq_send, dq_recv,
    root_part, root_recv, root_all, branch_all, slope_root, slope_branch, grads,
    load_sem, q_ss, q_rs, g_ss, g_rs, st_ss, st_rs, at_ss, at_rs, dq_ss, dq_rs,
    rs_ss, rs_rs, x_ss, x_rs, hd_ss, hd_rs, br_ss, br_rs,
):
    n, heads, branches = sizes
    me, my_head, my_branch = (
        lax.axis_index("seq"), lax.axis_index("head"), lax.axis_index("branch")
    )
    own, width = q_hbm.shape
    answers, per = att_out.shape[1:3]
    padded = qbuf.shape[0]
    chunks = padded // ROWS
    root_rows, branch_rows = rk_hbm.shape[0], bk_hbm.shape[1]
    piece = root_rows // heads
    scale = 1.0 / math.sqrt(width)

    def seq_to(d):
        return {"seq": lax.rem(me + d, n)}

    def seq_from(d):
        return lax.rem(me - d + n, n)

    def head_to(d):
        return {"head": lax.rem(my_head + d, heads)}

    def head_from(d):
        return lax.rem(my_head - d + heads, heads)

    def branch_to(d):
        return {"branch": lax.rem(my_branch + d, branches)}

    def branch_from(d):
        return lax.rem(my_branch - d + branches, branches)

    barrier = pltpu.get_barrier_semaphore()
    for to, count in ((seq_to, n), (head_to, heads), (branch_to, branches)):
        for d in range(1, count):
            pl.semaphore_signal(
                barrier, inc=1, device_id=to(d), device_id_type=pl.DeviceIdType.MESH
            )

    mine = pl.ds(pl.multiple_of(me * own, 16), own)
    loads = [
        pltpu.make_async_copy(q_hbm, qbuf.at[mine], load_sem.at[4]),
        pltpu.make_async_copy(g_hbm, gbuf.at[mine], load_sem.at[5]),
        pltpu.make_async_copy(pos_hbm, pos_ref, load_sem.at[6]),
        pltpu.make_async_copy(rk_hbm, keys.at[pl.ds(0, root_rows)], load_sem.at[0]),
        pltpu.make_async_copy(bk_hbm.at[0], keys.at[pl.ds(root_rows, branch_rows)], load_sem.at[1]),
        pltpu.make_async_copy(rv_hbm, values.at[pl.ds(0, root_rows)], load_sem.at[2]),
        pltpu.make_async_copy(bv_hbm.at[0], values.at[pl.ds(root_rows, branch_rows)], load_sem.at[3]),
    ]
    for load in loads:
        load.start()

    if padded > n * own:
        for target in (qbuf, gbuf):
            target[n * own:, :] = jnp.zeros((padded - n * own, width), BF16)

    pl.semaphore_wait(barrier, (n - 1) + (heads - 1) + (branches - 1))

    sends = []

    def send(*pieces):
        copy = remote(*pieces)
        copy.start()
        sends.append(copy)

    for rows, buf, ss, rs in ((q_hbm, qbuf, q_ss, q_rs), (g_hbm, gbuf, g_ss, g_rs)):
        for d in range(1, n):
            send(rows, buf.at[mine], ss.at[d - 1], rs.at[d - 1], seq_to(d))

    def arrived_rows(buf, ss, rs):
        for d in range(1, n):
            rows = pl.ds(pl.multiple_of(seq_from(d) * own, 16), own)
            remote(buf.at[rows], buf.at[rows], ss.at[d - 1], rs.at[d - 1], seq_to(d)).wait_recv()

    loads[2].wait()
    total = pos_ref.shape[1]
    spot = jnp.broadcast_to(pos_ref[...], (8, total))
    high = (spot >> 7).astype(F32).astype(BF16)
    low = (spot & 127).astype(F32).astype(BF16)

    def expand(c):
        row = lax.broadcasted_iota(jnp.int32, (total, ROWS), 1) + c * ROWS
        answer = lax.broadcasted_iota(jnp.int32, (total, ROWS), 0)
        pick = (row >= answer * per) & (row < answer * per + per)
        pick = jnp.where(pick, 1.0, 0.0).astype(BF16)
        place[c] = dot_plain(high, pick) * 128.0 + dot_plain(low, pick)

    over(chunks, expand)

    for load in loads[:2] + loads[3:]:
        load.wait()
    arrived_rows(qbuf, q_ss, q_rs)

    key_place = (
        lax.broadcasted_iota(jnp.int32, (branch_rows, ROWS), 0) + me * branch_rows
    ).astype(F32)

    def rows_of(c):
        return pl.ds(c * ROWS if isinstance(c, int) else pl.multiple_of(c * ROWS, ROWS), ROWS)

    def scores(c):
        q = qbuf[rows_of(c), :]
        on_root = dot_last(keys[:root_rows, :], q) * scale
        on_branch = dot_last(keys[root_rows:, :], q) * scale
        on_branch = jnp.where(key_place <= place[c, 0:1, :], on_branch, NEG)
        peak = jnp.maximum(
            jnp.max(on_root, axis=0, keepdims=True), jnp.max(on_branch, axis=0, keepdims=True)
        )
        p_root = jnp.exp(on_root - peak)
        p_branch = jnp.exp(on_branch - peak)
        probs[c, :root_rows, :] = p_root
        probs[c, root_rows:, :] = p_branch
        sums = jnp.sum(p_root, axis=0, keepdims=True) + jnp.sum(p_branch, axis=0, keepdims=True)
        share = dot_first(values[:root_rows, :], p_root.astype(BF16))
        share = share + dot_first(values[root_rows:, :], p_branch.astype(BF16))
        weighted[c] = share
        stats[me, c, 0:1, :] = peak
        stats[me, c, 1:2, :] = sums

    over(chunks, scores)
    arrived_rows(gbuf, g_ss, g_rs)

    def dots(c):
        turned = gbuf[rows_of(c), :].astype(F32).T
        stats[me, c, 2:3, :] = jnp.sum(weighted[c] * turned, axis=0, keepdims=True)
        stats[me, c, 3:8, :] = jnp.zeros((5, ROWS), F32)

    over(chunks, dots)
    for d in range(1, n):
        send(stats.at[me], stats.at[me], st_ss.at[d - 1], st_rs.at[d - 1], seq_to(d))

    def products(c):
        g = gbuf[rows_of(c), :]
        product[c, :root_rows, :] = dot_last(values[:root_rows, :], g)
        product[c, root_rows:, :] = dot_last(values[root_rows:, :], g)

    over(chunks, products)
    for d in range(1, n):
        at = seq_from(d)
        remote(stats.at[at], stats.at[at], st_ss.at[d - 1], st_rs.at[d - 1], seq_to(d)).wait_recv()

    def combine(c):
        peak = stats[0, c, 0:1, :]
        for s in range(1, n):
            peak = jnp.maximum(peak, stats[s, c, 0:1, :])
        sums, dotted = jnp.zeros((1, ROWS), F32), jnp.zeros((1, ROWS), F32)
        for s in range(n):
            factor = jnp.exp(stats[s, c, 0:1, :] - peak)
            sums = sums + stats[s, c, 1:2, :] * factor
            dotted = dotted + stats[s, c, 2:3, :] * factor
        factor = jnp.exp(stats[me, c, 0:1, :] - peak) / sums
        place[c, 1:2, :] = factor
        place[c, 2:3, :] = dotted / sums

    over(chunks, combine)

    def value_term(c, start, count, slope):
        weights = probs[c, start:start + count, :] * place[c, 1:2, :]
        return dot_plain(weights.astype(BF16), gbuf[rows_of(c), :])

    def key_term(c, start, count, slope):
        weights = probs[c, start:start + count, :] * place[c, 1:2, :]
        gap = product[c, start:start + count, :] - place[c, 2:3, :]
        sloped = (weights * gap).astype(BF16)
        slope[c] = sloped
        return dot_plain(sloped, qbuf[rows_of(c), :]) * scale

    def sweep(term, start, count, slope):
        if chunks == 1:
            return term(0, start, count, slope)
        grads[:count, :] = jnp.zeros((count, width), F32)

        def add(c):
            grads[:count, :] += term(c, start, count, slope)

        over(chunks, add)
        return grads[:count, :]

    for at, term in enumerate((value_term, key_term)):
        root_part[at] = sweep(term, 0, root_rows, slope_root).astype(BF16)
        for d in range(1, heads):
            far = pl.ds(pl.multiple_of(lax.rem(my_head + d, heads) * piece, 16), piece)
            send(
                root_part.at[at, far], root_recv.at[at, d - 1],
                rs_ss.at[at, d - 1], rs_rs.at[at, d - 1], head_to(d),
            )

    near = pl.ds(pl.multiple_of(my_head * piece, 16), piece)
    for at in range(2):
        term = root_part[at, near, :].astype(F32)
        for d in range(1, heads):
            remote(
                root_recv.at[at, d - 1], root_recv.at[at, d - 1],
                rs_ss.at[at, d - 1], rs_rs.at[at, d - 1], head_to(d),
            ).wait_recv()
            term = term + root_recv[at, d - 1].astype(F32)
        root_all[at, my_branch, my_head] = term.astype(BF16)
        block = root_all.at[at, my_branch, my_head]
        for d in range(1, branches):
            send(block, block, x_ss.at[at, d - 1], x_rs.at[at, d - 1], branch_to(d))
        for d in range(1, heads):
            send(block, block, hd_ss.at[at, 0, d - 1], hd_rs.at[at, 0, d - 1], head_to(d))

    for at, term in enumerate((value_term, key_term)):
        branch_all[at, my_head] = sweep(term, root_rows, branch_rows, slope_branch).astype(BF16)
        block = branch_all.at[at, my_head]
        for d in range(1, heads):
            send(block, block, br_ss.at[at, d - 1], br_rs.at[at, d - 1], head_to(d))

    def forward(at):
        for d in range(1, branches):
            block = root_all.at[at, branch_from(d), my_head]
            remote(block, block, x_ss.at[at, d - 1], x_rs.at[at, d - 1], branch_to(d)).wait_recv()
            for e in range(1, heads):
                send(block, block, hd_ss.at[at, d, e - 1], hd_rs.at[at, d, e - 1], head_to(e))

    forward(0)

    def query_terms(c):
        term = dot_first(slope_root[c], keys[:root_rows, :])
        term = term + dot_first(slope_branch[c], keys[root_rows:, :])
        dq_send[rows_of(c), :] = (term * scale).astype(BF16)
        att_send[rows_of(c), :] = (weighted[c] * place[c, 1:2, :]).T.astype(BF16)

    over(chunks, query_terms)
    for buf, into, ss, rs in ((dq_send, dq_recv, dq_ss, dq_rs), (att_send, att_recv, at_ss, at_rs)):
        for d in range(1, n):
            far = pl.ds(pl.multiple_of(lax.rem(me + d, n) * own, 16), own)
            send(buf.at[far], into.at[d - 1], ss.at[d - 1], rs.at[d - 1], seq_to(d))

    forward(1)

    for at, out in ((0, bv_out), (1, bk_out)):
        for d in range(1, heads):
            block = branch_all.at[at, head_from(d)]
            remote(block, block, br_ss.at[at, d - 1], br_rs.at[at, d - 1], head_to(d)).wait_recv()
        term = branch_all[at, 0].astype(F32)
        for h in range(1, heads):
            term = term + branch_all[at, h].astype(F32)
        out[0] = term

    for at, (buf, into, ss, rs, out) in enumerate((
        (dq_send, dq_recv, dq_ss, dq_rs, dq_out), (att_send, att_recv, at_ss, at_rs, att_out)
    )):
        term = buf[mine, :].astype(F32)
        for d in range(1, n):
            remote(
                into.at[d - 1], into.at[d - 1], ss.at[d - 1], rs.at[d - 1], seq_to(d)
            ).wait_recv()
            term = term + into[d - 1].astype(F32)
        rows_f32[at] = term
        for i in range(answers):
            out[0, i] = rows_f32[at, i * per:(i + 1) * per, :].astype(out.dtype)

    for at, out in ((0, rv_out), (1, rk_out)):
        for b in range(branches):
            for d in range(1, heads):
                block = root_all.at[at, lax.rem(my_branch - b + branches, branches), head_from(d)]
                remote(
                    block, block, hd_ss.at[at, b, d - 1], hd_rs.at[at, b, d - 1], head_to(d)
                ).wait_recv()
        for h in range(heads):
            term = root_all[at, 0, h].astype(F32)
            for b in range(1, branches):
                term = term + root_all[at, b, h].astype(F32)
            out[h * piece:(h + 1) * piece, :] = term

    for copy in sends:
        copy.wait_send()


def hand_out(*refs):
    sems = refs[12]
    copies = [pltpu.make_async_copy(refs[i], refs[6 + i], sems.at[i]) for i in range(6)]
    for copy in copies:
        copy.start()
    for copy in copies:
        copy.wait()


def per_device(sizes, queries, output_cotangent, root_keys, root_values, branch_keys,
               branch_values, answer_positions):
    n, heads, branches = sizes
    answers, per, width = queries.shape[1:]
    own = answers * per
    padded = -(-n * own // ROWS) * ROWS
    chunks = padded // ROWS
    root_rows, branch_rows = root_keys.shape[0], branch_keys.shape[1]
    key_rows = root_rows + branch_rows
    piece = root_rows // heads
    vmem = pl.BlockSpec(memory_space=pltpu.VMEM)
    whole = pl.BlockSpec(memory_space=pltpu.HBM)

    def sem(*shape):
        return pltpu.SemaphoreType.DMA(tuple(max(1, size) for size in shape))

    z, h, b = max(1, n - 1), max(1, heads - 1), max(1, branches - 1)
    scratch = [
        pltpu.VMEM(answer_positions.shape, jnp.int32),
        pltpu.VMEM((key_rows, width), BF16),
        pltpu.VMEM((key_rows, width), BF16),
        pltpu.VMEM((2, own, width), F32),
        pltpu.VMEM((padded, width), BF16),
        pltpu.VMEM((padded, width), BF16),
        pltpu.VMEM((n, chunks, 8, ROWS), F32),
        pltpu.VMEM((chunks, key_rows, ROWS), F32),
        pltpu.VMEM((chunks, key_rows, ROWS), F32),
        pltpu.VMEM((chunks, width, ROWS), F32),
        pltpu.VMEM((chunks, 8, ROWS), F32),
        pltpu.VMEM((padded, width), BF16),
        pltpu.VMEM((z, own, width), BF16),
        pltpu.VMEM((8, 128), F32),
        pltpu.VMEM((padded, width), BF16),
        pltpu.VMEM((z, own, width), BF16),
        pltpu.VMEM((2, root_rows, width), BF16),
        pltpu.VMEM((2, h, piece, width), BF16),
        pltpu.VMEM((2, branches, heads, piece, width), BF16),
        pltpu.VMEM((2, heads, branch_rows, width), BF16),
        pltpu.VMEM((chunks, root_rows, ROWS), BF16),
        pltpu.VMEM((chunks, branch_rows, ROWS), BF16),
        pltpu.VMEM((max(root_rows, branch_rows), width), F32),
        sem(7),
        sem(z), sem(z), sem(z), sem(z), sem(z), sem(z), sem(z), sem(z), sem(z), sem(z),
        sem(2, h), sem(2, h), sem(2, b), sem(2, b),
        sem(2, branches, h), sem(2, branches, h), sem(2, h), sem(2, h),
    ]
    outs = (
        jax.ShapeDtypeStruct(queries.shape, BF16),
        jax.ShapeDtypeStruct(queries.shape, F32),
        jax.ShapeDtypeStruct(root_keys.shape, F32),
        jax.ShapeDtypeStruct(root_values.shape, F32),
        jax.ShapeDtypeStruct(branch_keys.shape, F32),
        jax.ShapeDtypeStruct(branch_values.shape, F32),
    )
    results = pl.pallas_call(
        functools.partial(kernel, sizes),
        out_shape=outs,
        in_specs=[whole] * 7,
        out_specs=[vmem] * 6,
        scratch_shapes=scratch,
        compiler_params=pltpu.CompilerParams(
            collective_id=0, has_side_effects=True, vmem_limit_bytes=48 * 1024 * 1024
        ),
    )(*(
        pltpu.with_memory_space_constraint(array, pltpu.HBM) for array in (
            queries.reshape(own, width), output_cotangent.reshape(own, width),
            answer_positions, root_keys, root_values,
            branch_keys, branch_values,
        )
    ))
    return pl.pallas_call(
        hand_out,
        out_shape=outs,
        in_specs=[vmem] * 6,
        out_specs=[whole] * 6,
        scratch_shapes=[pltpu.SemaphoreType.DMA((6,))],
        compiler_params=pltpu.CompilerParams(vmem_limit_bytes=2 * 1024 * 1024),
    )(*results)


def solution(mesh):
    sizes = (mesh.shape["seq"], mesh.shape["head"], mesh.shape["branch"])
    rows = P(("parts", "branch"), "seq", "head", None)
    root = P(("parts", "seq"), None)
    branch = P(("parts", "branch"), "seq", None)
    return jax.shard_map(
        functools.partial(per_device, sizes),
        mesh=mesh,
        in_specs=(rows, rows, root, root, branch, branch, P(("parts", "branch"), None)),
        out_specs=(rows, rows, root, root, branch, branch),
        check_vma=False,
    )
```

```python
import functools
import math

import jax
import jax.numpy as jnp
from jax import lax
from jax.experimental import pallas as pl
from jax.experimental.pallas import tpu as pltpu
from jax.sharding import PartitionSpec as P

NEG = -1e30
ROWS = 256
F32 = jnp.float32
BF16 = jnp.bfloat16


def dot_last(left, right):
    return lax.dot_general(left, right, (((1,), (1,)), ((), ())), preferred_element_type=F32)


def dot_plain(left, right):
    return jnp.dot(left, right, preferred_element_type=F32)


def remote(src, dst, send, recv, device):
    return pltpu.make_async_remote_copy(
        src_ref=src,
        dst_ref=dst,
        send_sem=send,
        recv_sem=recv,
        device_id=device,
        device_id_type=pl.DeviceIdType.MESH,
    )


def over(count, body):
    if count == 1:
        body(0)
    else:
        lax.fori_loop(0, count, lambda at, carry: (body(at), carry)[1], 0)


def kernel(
    sizes,
    q_hbm, g_hbm, pos_hbm, rk_hbm, rv_hbm, bk_hbm, bv_hbm,
    att_out, dq_out, rk_out, rv_out, bk_out, bv_out,
    pos_ref, keys, values, keys_t, values_t, rows_f32, qbuf, gbuf, stats, probs, product, weighted, place,
    att_send, att_recv, near, dq_send, dq_recv,
    root_part, root_recv, root_all, branch_all, slope, grads,
    load_sem, q_ss, q_rs, g_ss, g_rs, st_ss, st_rs, at_ss, at_rs, dq_ss, dq_rs,
    rs_ss, rs_rs, x_ss, x_rs, hd_ss, hd_rs, br_ss, br_rs,
):
    n, heads, branches = sizes
    me, my_head, my_branch = (
        lax.axis_index("seq"), lax.axis_index("head"), lax.axis_index("branch")
    )
    own, width = q_hbm.shape
    answers, per = att_out.shape[1:3]
    padded = qbuf.shape[0]
    chunks = padded // ROWS
    root_rows, branch_rows = rk_hbm.shape[0], bk_hbm.shape[1]
    piece = root_rows // heads
    scale = 1.0 / math.sqrt(width)

    def seq_to(d):
        return {"seq": lax.rem(me + d, n)}

    def seq_from(d):
        return lax.rem(me - d + n, n)

    def head_to(d):
        return {"head": lax.rem(my_head + d, heads)}

    def head_from(d):
        return lax.rem(my_head - d + heads, heads)

    def branch_to(d):
        return {"branch": lax.rem(my_branch + d, branches)}

    def branch_from(d):
        return lax.rem(my_branch - d + branches, branches)

    barrier = pltpu.get_barrier_semaphore()
    for to, count in ((seq_to, n), (head_to, heads), (branch_to, branches)):
        for d in range(1, count):
            pl.semaphore_signal(
                barrier, inc=1, device_id=to(d), device_id_type=pl.DeviceIdType.MESH
            )

    mine = pl.ds(pl.multiple_of(me * own, 16), own)
    pl.semaphore_wait(barrier, (n - 1) + (heads - 1) + (branches - 1))

    sends = []

    def send(*pieces):
        copy = remote(*pieces)
        copy.start()
        sends.append(copy)

    for rows, buf, ss, rs in ((q_hbm, qbuf, q_ss, q_rs), (g_hbm, gbuf, g_ss, g_rs)):
        for d in range(1, n):
            send(rows, buf.at[mine], ss.at[d - 1], rs.at[d - 1], seq_to(d))

    loads = [
        pltpu.make_async_copy(q_hbm, qbuf.at[mine], load_sem.at[4]),
        pltpu.make_async_copy(g_hbm, gbuf.at[mine], load_sem.at[5]),
        pltpu.make_async_copy(pos_hbm, pos_ref, load_sem.at[6]),
        pltpu.make_async_copy(rk_hbm, keys.at[pl.ds(0, root_rows)], load_sem.at[0]),
        pltpu.make_async_copy(bk_hbm.at[0], keys.at[pl.ds(root_rows, branch_rows)], load_sem.at[1]),
        pltpu.make_async_copy(rv_hbm, values.at[pl.ds(0, root_rows)], load_sem.at[2]),
        pltpu.make_async_copy(bv_hbm.at[0], values.at[pl.ds(root_rows, branch_rows)], load_sem.at[3]),
    ]
    for load in loads:
        load.start()

    if padded > n * own:
        for target in (qbuf, gbuf):
            target[n * own:, :] = jnp.zeros((padded - n * own, width), BF16)

    def arrived_rows(buf, ss, rs):
        for d in range(1, n):
            rows = pl.ds(pl.multiple_of(seq_from(d) * own, 16), own)
            remote(buf.at[rows], buf.at[rows], ss.at[d - 1], rs.at[d - 1], seq_to(d)).wait_recv()

    loads[2].wait()
    total = pos_ref.shape[1]
    spot = jnp.broadcast_to(pos_ref[...], (8, total))
    high = (spot >> 7).astype(F32).astype(BF16)
    low = (spot & 127).astype(F32).astype(BF16)

    def expand(c):
        row = lax.broadcasted_iota(jnp.int32, (total, ROWS), 1) + c * ROWS
        answer = lax.broadcasted_iota(jnp.int32, (total, ROWS), 0)
        pick = (row >= answer * per) & (row < answer * per + per)
        pick = jnp.where(pick, 1.0, 0.0).astype(BF16)
        place[c] = dot_plain(high, pick) * 128.0 + dot_plain(low, pick)

    over(chunks, expand)

    for load in loads[3:]:
        load.wait()
    keys_t[...] = keys[...].astype(F32).T.astype(BF16)
    values_t[...] = values[...].astype(F32).T.astype(BF16)
    for load in loads[:2]:
        load.wait()
    arrived_rows(qbuf, q_ss, q_rs)

    key_place = (
        lax.broadcasted_iota(jnp.int32, (branch_rows, ROWS), 0) + me * branch_rows
    ).astype(F32)

    def rows_of(c):
        return pl.ds(c * ROWS if isinstance(c, int) else pl.multiple_of(c * ROWS, ROWS), ROWS)

    def scores(c):
        q = qbuf[rows_of(c), :]
        on_root = dot_last(keys[:root_rows, :], q) * scale
        on_branch = dot_last(keys[root_rows:, :], q) * scale
        on_branch = jnp.where(key_place <= place[c, 0:1, :], on_branch, NEG)
        peak = jnp.maximum(
            jnp.max(on_root, axis=0, keepdims=True), jnp.max(on_branch, axis=0, keepdims=True)
        )
        p_root = jnp.exp(on_root - peak)
        p_branch = jnp.exp(on_branch - peak)
        probs[c, :root_rows, :] = p_root
        probs[c, root_rows:, :] = p_branch
        sums = jnp.sum(p_root, axis=0, keepdims=True) + jnp.sum(p_branch, axis=0, keepdims=True)
        share = dot_plain(values_t[:, :root_rows], p_root.astype(BF16))
        share = share + dot_plain(values_t[:, root_rows:], p_branch.astype(BF16))
        weighted[c] = share
        stats[me, c, 0:1, :] = peak
        stats[me, c, 1:2, :] = sums

    over(chunks, scores)
    arrived_rows(gbuf, g_ss, g_rs)

    def dots(c):
        turned = gbuf[rows_of(c), :].astype(F32).T
        stats[me, c, 2:3, :] = jnp.sum(weighted[c] * turned, axis=0, keepdims=True)
        stats[me, c, 3:8, :] = jnp.zeros((5, ROWS), F32)

    over(chunks, dots)
    for d in range(1, n):
        send(stats.at[me], stats.at[me], st_ss.at[d - 1], st_rs.at[d - 1], seq_to(d))

    def products(c):
        g = gbuf[rows_of(c), :]
        product[c, :root_rows, :] = dot_last(values[:root_rows, :], g)
        product[c, root_rows:, :] = dot_last(values[root_rows:, :], g)

    over(chunks, products)
    for d in range(1, n):
        at = seq_from(d)
        remote(stats.at[at], stats.at[at], st_ss.at[d - 1], st_rs.at[d - 1], seq_to(d)).wait_recv()

    def combine(c):
        peak = stats[0, c, 0:1, :]
        for s in range(1, n):
            peak = jnp.maximum(peak, stats[s, c, 0:1, :])
        sums, dotted = jnp.zeros((1, ROWS), F32), jnp.zeros((1, ROWS), F32)
        for s in range(n):
            factor = jnp.exp(stats[s, c, 0:1, :] - peak)
            sums = sums + stats[s, c, 1:2, :] * factor
            dotted = dotted + stats[s, c, 2:3, :] * factor
        factor = jnp.exp(stats[me, c, 0:1, :] - peak) / sums
        place[c, 1:2, :] = factor
        place[c, 2:3, :] = dotted / sums

    over(chunks, combine)

    def value_term(c, span):
        weights = probs[c, span, :] * place[c, 1:2, :]
        return dot_plain(weights.astype(BF16), gbuf[rows_of(c), :])

    def key_term(c, span):
        weights = probs[c, span, :] * place[c, 1:2, :]
        gap = product[c, span, :] - place[c, 2:3, :]
        sloped = (weights * gap).astype(BF16)
        slope[c, span, :] = sloped
        return dot_plain(sloped, qbuf[rows_of(c), :]) * scale

    def sweep(term, start, count):
        span = pl.ds(start, count)
        if chunks == 1:
            return term(0, span)
        grads[:count, :] = jnp.zeros((count, width), F32)

        def add(c):
            grads[:count, :] += term(c, span)

        over(chunks, add)
        return grads[:count, :]

    def piece_start(d):
        return pl.multiple_of(lax.rem(my_head + d, heads) * piece, 16)

    def far_pieces(at, term):
        for d in range(1, heads):
            root_part[at, d - 1] = sweep(term, piece_start(d), piece).astype(BF16)
            send(
                root_part.at[at, d - 1], root_recv.at[at, d - 1],
                rs_ss.at[at, d - 1], rs_rs.at[at, d - 1], head_to(d),
            )

    def near_piece(at, term):
        near[at] = sweep(term, piece_start(0), piece)

    def spread(at):
        term = near[at]
        for d in range(1, heads):
            remote(
                root_recv.at[at, d - 1], root_recv.at[at, d - 1],
                rs_ss.at[at, d - 1], rs_rs.at[at, d - 1], head_to(d),
            ).wait_recv()
            term = term + root_recv[at, d - 1].astype(F32)
        root_all[at, my_branch, my_head] = term.astype(BF16)
        block = root_all.at[at, my_branch, my_head]
        for d in range(1, branches):
            send(block, block, x_ss.at[at, d - 1], x_rs.at[at, d - 1], branch_to(d))
        for d in range(1, heads):
            send(block, block, hd_ss.at[at, 0, d - 1], hd_rs.at[at, 0, d - 1], head_to(d))

    far_pieces(0, value_term)
    near_piece(0, value_term)
    far_pieces(1, key_term)
    spread(0)
    near_piece(1, key_term)
    spread(1)

    for at, term in enumerate((value_term, key_term)):
        branch_all[at, my_head] = sweep(term, root_rows, branch_rows).astype(BF16)
        block = branch_all.at[at, my_head]
        for d in range(1, heads):
            send(block, block, br_ss.at[at, d - 1], br_rs.at[at, d - 1], head_to(d))

    def share_rows(buf, into, ss, rs):
        for d in range(1, n):
            far = pl.ds(pl.multiple_of(lax.rem(me + d, n) * own, 16), own)
            send(buf.at[far], into.at[d - 1], ss.at[d - 1], rs.at[d - 1], seq_to(d))

    def query_terms(c):
        term = dot_plain(keys_t[...], slope[c]) * scale
        dq_send[rows_of(c), :] = term.T.astype(BF16)

    def shares(c):
        att_send[rows_of(c), :] = (weighted[c] * place[c, 1:2, :]).T.astype(BF16)

    over(chunks, query_terms)
    share_rows(dq_send, dq_recv, dq_ss, dq_rs)
    over(chunks, shares)
    share_rows(att_send, att_recv, at_ss, at_rs)

    def forward(at):
        for d in range(1, branches):
            block = root_all.at[at, branch_from(d), my_head]
            remote(block, block, x_ss.at[at, d - 1], x_rs.at[at, d - 1], branch_to(d)).wait_recv()
            for e in range(1, heads):
                send(block, block, hd_ss.at[at, d, e - 1], hd_rs.at[at, d, e - 1], head_to(e))

    for at, out in ((0, bv_out), (1, bk_out)):
        for d in range(1, heads):
            block = branch_all.at[at, head_from(d)]
            remote(block, block, br_ss.at[at, d - 1], br_rs.at[at, d - 1], head_to(d)).wait_recv()
        term = branch_all[at, 0].astype(F32)
        for h in range(1, heads):
            term = term + branch_all[at, h].astype(F32)
        out[0] = term

    forward(0)
    forward(1)

    for at, (buf, into, ss, rs, out) in enumerate((
        (dq_send, dq_recv, dq_ss, dq_rs, dq_out), (att_send, att_recv, at_ss, at_rs, att_out)
    )):
        term = buf[mine, :].astype(F32)
        for d in range(1, n):
            remote(
                into.at[d - 1], into.at[d - 1], ss.at[d - 1], rs.at[d - 1], seq_to(d)
            ).wait_recv()
            term = term + into[d - 1].astype(F32)
        rows_f32[at] = term
        for i in range(answers):
            out[0, i] = rows_f32[at, i * per:(i + 1) * per, :].astype(out.dtype)

    for at, out in ((0, rv_out), (1, rk_out)):
        for b in range(branches):
            for d in range(1, heads):
                block = root_all.at[at, lax.rem(my_branch - b + branches, branches), head_from(d)]
                remote(
                    block, block, hd_ss.at[at, b, d - 1], hd_rs.at[at, b, d - 1], head_to(d)
                ).wait_recv()
        for h in range(heads):
            term = root_all[at, 0, h].astype(F32)
            for b in range(1, branches):
                term = term + root_all[at, b, h].astype(F32)
            out[h * piece:(h + 1) * piece, :] = term

    for copy in sends:
        copy.wait_send()


def hand_out(*refs):
    sems = refs[12]
    copies = [pltpu.make_async_copy(refs[i], refs[6 + i], sems.at[i]) for i in range(6)]
    for copy in copies:
        copy.start()
    for copy in copies:
        copy.wait()


def per_device(sizes, queries, output_cotangent, root_keys, root_values, branch_keys,
               branch_values, answer_positions):
    n, heads, branches = sizes
    answers, per, width = queries.shape[1:]
    own = answers * per
    padded = -(-n * own // ROWS) * ROWS
    chunks = padded // ROWS
    root_rows, branch_rows = root_keys.shape[0], branch_keys.shape[1]
    key_rows = root_rows + branch_rows
    piece = root_rows // heads
    vmem = pl.BlockSpec(memory_space=pltpu.VMEM)
    whole = pl.BlockSpec(memory_space=pltpu.HBM)

    def sem(*shape):
        return pltpu.SemaphoreType.DMA(tuple(max(1, size) for size in shape))

    z, h, b = max(1, n - 1), max(1, heads - 1), max(1, branches - 1)
    scratch = [
        pltpu.VMEM(answer_positions.shape, jnp.int32),
        pltpu.VMEM((key_rows, width), BF16),
        pltpu.VMEM((key_rows, width), BF16),
        pltpu.VMEM((width, key_rows), BF16),
        pltpu.VMEM((width, key_rows), BF16),
        pltpu.VMEM((2, own, width), F32),
        pltpu.VMEM((padded, width), BF16),
        pltpu.VMEM((padded, width), BF16),
        pltpu.VMEM((n, chunks, 8, ROWS), F32),
        pltpu.VMEM((chunks, key_rows, ROWS), F32),
        pltpu.VMEM((chunks, key_rows, ROWS), F32),
        pltpu.VMEM((chunks, width, ROWS), F32),
        pltpu.VMEM((chunks, 8, ROWS), F32),
        pltpu.VMEM((padded, width), BF16),
        pltpu.VMEM((z, own, width), BF16),
        pltpu.VMEM((2, piece, width), F32),
        pltpu.VMEM((padded, width), BF16),
        pltpu.VMEM((z, own, width), BF16),
        pltpu.VMEM((2, h, piece, width), BF16),
        pltpu.VMEM((2, h, piece, width), BF16),
        pltpu.VMEM((2, branches, heads, piece, width), BF16),
        pltpu.VMEM((2, heads, branch_rows, width), BF16),
        pltpu.VMEM((chunks, key_rows, ROWS), BF16),
        pltpu.VMEM((max(root_rows, branch_rows), width), F32),
        sem(7),
        sem(z), sem(z), sem(z), sem(z), sem(z), sem(z), sem(z), sem(z), sem(z), sem(z),
        sem(2, h), sem(2, h), sem(2, b), sem(2, b),
        sem(2, branches, h), sem(2, branches, h), sem(2, h), sem(2, h),
    ]
    outs = (
        jax.ShapeDtypeStruct(queries.shape, BF16),
        jax.ShapeDtypeStruct(queries.shape, F32),
        jax.ShapeDtypeStruct(root_keys.shape, F32),
        jax.ShapeDtypeStruct(root_values.shape, F32),
        jax.ShapeDtypeStruct(branch_keys.shape, F32),
        jax.ShapeDtypeStruct(branch_values.shape, F32),
    )
    results = pl.pallas_call(
        functools.partial(kernel, sizes),
        out_shape=outs,
        in_specs=[whole] * 7,
        out_specs=[vmem] * 6,
        scratch_shapes=scratch,
        compiler_params=pltpu.CompilerParams(
            collective_id=0, has_side_effects=True, vmem_limit_bytes=48 * 1024 * 1024
        ),
    )(*(
        pltpu.with_memory_space_constraint(array, pltpu.HBM) for array in (
            queries.reshape(own, width), output_cotangent.reshape(own, width),
            answer_positions, root_keys, root_values,
            branch_keys, branch_values,
        )
    ))
    return pl.pallas_call(
        hand_out,
        out_shape=outs,
        in_specs=[vmem] * 6,
        out_specs=[whole] * 6,
        scratch_shapes=[pltpu.SemaphoreType.DMA((6,))],
        compiler_params=pltpu.CompilerParams(vmem_limit_bytes=2 * 1024 * 1024),
    )(*results)


def solution(mesh):
    sizes = (mesh.shape["seq"], mesh.shape["head"], mesh.shape["branch"])
    rows = P(("parts", "branch"), "seq", "head", None)
    root = P(("parts", "seq"), None)
    branch = P(("parts", "branch"), "seq", None)
    return jax.shard_map(
        functools.partial(per_device, sizes),
        mesh=mesh,
        in_specs=(rows, rows, root, root, branch, branch, P(("parts", "branch"), None)),
        out_specs=(rows, rows, root, root, branch, branch),
        check_vma=False,
    )
```

```python
import functools
import math

import jax
import jax.numpy as jnp
from jax import lax
from jax.experimental import pallas as pl
from jax.experimental.pallas import tpu as pltpu
from jax.sharding import PartitionSpec as P

NEG = -1e30
ROWS = 256
F32 = jnp.float32
BF16 = jnp.bfloat16


def dot_last(left, right):
    return lax.dot_general(left, right, (((1,), (1,)), ((), ())), preferred_element_type=F32)


def dot_plain(left, right):
    return jnp.dot(left, right, preferred_element_type=F32)


def remote(src, dst, send, recv, device):
    return pltpu.make_async_remote_copy(
        src_ref=src,
        dst_ref=dst,
        send_sem=send,
        recv_sem=recv,
        device_id=device,
        device_id_type=pl.DeviceIdType.MESH,
    )


def over(count, body):
    if count == 1:
        body(0)
    else:
        lax.fori_loop(0, count, lambda at, carry: (body(at), carry)[1], 0)


def kernel(
    sizes,
    q_hbm, g_hbm, pos_hbm, rk_hbm, rv_hbm, bk_hbm, bv_hbm,
    att_out, dq_out, rk_out, rv_out, bk_out, bv_out,
    pos_ref, keys, values, keys_t, values_t, rows_f32, qbuf, gbuf, stats, probs, product, weighted, place,
    att_send, att_recv, near, dq_send, dq_recv,
    root_part, root_recv, root_all, branch_all, slope, grads,
    load_sem, q_ss, q_rs, g_ss, g_rs, st_ss, st_rs, at_ss, at_rs, dq_ss, dq_rs,
    rs_ss, rs_rs, x_ss, x_rs, hd_ss, hd_rs, br_ss, br_rs,
):
    n, heads, branches = sizes
    me, my_head, my_branch = (
        lax.axis_index("seq"), lax.axis_index("head"), lax.axis_index("branch")
    )
    own, width = q_hbm.shape
    answers, per = att_out.shape[1:3]
    padded = qbuf.shape[0]
    chunks = padded // ROWS
    root_rows, branch_rows = rk_hbm.shape[0], bk_hbm.shape[1]
    piece = root_rows // heads
    scale = 1.0 / math.sqrt(width)

    def seq_to(d):
        return {"seq": lax.rem(me + d, n)}

    def seq_from(d):
        return lax.rem(me - d + n, n)

    def head_to(d):
        return {"head": lax.rem(my_head + d, heads)}

    def head_from(d):
        return lax.rem(my_head - d + heads, heads)

    def branch_to(d):
        return {"branch": lax.rem(my_branch + d, branches)}

    def branch_from(d):
        return lax.rem(my_branch - d + branches, branches)

    barrier = pltpu.get_barrier_semaphore()
    for to, count in ((seq_to, n), (head_to, heads), (branch_to, branches)):
        for d in range(1, count):
            pl.semaphore_signal(
                barrier, inc=1, device_id=to(d), device_id_type=pl.DeviceIdType.MESH
            )

    mine = pl.ds(pl.multiple_of(me * own, 16), own)
    loads = [
        pltpu.make_async_copy(q_hbm, qbuf.at[mine], load_sem.at[4]),
        pltpu.make_async_copy(g_hbm, gbuf.at[mine], load_sem.at[5]),
        pltpu.make_async_copy(pos_hbm, pos_ref, load_sem.at[6]),
        pltpu.make_async_copy(rk_hbm, keys.at[pl.ds(0, root_rows)], load_sem.at[0]),
        pltpu.make_async_copy(bk_hbm.at[0], keys.at[pl.ds(root_rows, branch_rows)], load_sem.at[1]),
        pltpu.make_async_copy(rv_hbm, values.at[pl.ds(0, root_rows)], load_sem.at[2]),
        pltpu.make_async_copy(bv_hbm.at[0], values.at[pl.ds(root_rows, branch_rows)], load_sem.at[3]),
    ]
    for load in loads:
        load.start()

    pl.semaphore_wait(barrier, (n - 1) + (heads - 1) + (branches - 1))

    sends = []

    def send(*pieces):
        copy = remote(*pieces)
        copy.start()
        sends.append(copy)

    for load, buf, ss, rs in ((loads[0], qbuf, q_ss, q_rs), (loads[1], gbuf, g_ss, g_rs)):
        load.wait()
        for d in range(1, n):
            send(buf.at[mine], buf.at[mine], ss.at[d - 1], rs.at[d - 1], seq_to(d))

    if padded > n * own:
        for target in (qbuf, gbuf):
            target[n * own:, :] = jnp.zeros((padded - n * own, width), BF16)

    def arrived_rows(buf, ss, rs):
        for d in range(1, n):
            rows = pl.ds(pl.multiple_of(seq_from(d) * own, 16), own)
            remote(buf.at[rows], buf.at[rows], ss.at[d - 1], rs.at[d - 1], seq_to(d)).wait_recv()

    loads[2].wait()
    total = pos_ref.shape[1]
    spot = jnp.broadcast_to(pos_ref[...], (8, total))
    high = (spot >> 7).astype(F32).astype(BF16)
    low = (spot & 127).astype(F32).astype(BF16)

    def expand(c):
        row = lax.broadcasted_iota(jnp.int32, (total, ROWS), 1) + c * ROWS
        answer = lax.broadcasted_iota(jnp.int32, (total, ROWS), 0)
        pick = (row >= answer * per) & (row < answer * per + per)
        pick = jnp.where(pick, 1.0, 0.0).astype(BF16)
        place[c] = dot_plain(high, pick) * 128.0 + dot_plain(low, pick)

    over(chunks, expand)

    for load in loads[3:]:
        load.wait()
    values_t[...] = values[...].astype(F32).T.astype(BF16)
    arrived_rows(qbuf, q_ss, q_rs)

    key_place = (
        lax.broadcasted_iota(jnp.int32, (branch_rows, ROWS), 0) + me * branch_rows
    ).astype(F32)

    def rows_of(c):
        return pl.ds(c * ROWS if isinstance(c, int) else pl.multiple_of(c * ROWS, ROWS), ROWS)

    def scores(c):
        q = qbuf[rows_of(c), :]
        on_root = dot_last(keys[:root_rows, :], q) * scale
        on_branch = dot_last(keys[root_rows:, :], q) * scale
        on_branch = jnp.where(key_place <= place[c, 0:1, :], on_branch, NEG)
        peak = jnp.maximum(
            jnp.max(on_root, axis=0, keepdims=True), jnp.max(on_branch, axis=0, keepdims=True)
        )
        p_root = jnp.exp(on_root - peak)
        p_branch = jnp.exp(on_branch - peak)
        probs[c, :root_rows, :] = p_root
        probs[c, root_rows:, :] = p_branch
        sums = jnp.sum(p_root, axis=0, keepdims=True) + jnp.sum(p_branch, axis=0, keepdims=True)
        share = dot_plain(values_t[:, :root_rows], p_root.astype(BF16))
        share = share + dot_plain(values_t[:, root_rows:], p_branch.astype(BF16))
        weighted[c] = share
        stats[me, c, 0:1, :] = peak
        stats[me, c, 1:2, :] = sums

    over(chunks, scores)
    arrived_rows(gbuf, g_ss, g_rs)

    def dots(c):
        turned = gbuf[rows_of(c), :].astype(F32).T
        stats[me, c, 2:3, :] = jnp.sum(weighted[c] * turned, axis=0, keepdims=True)
        stats[me, c, 3:8, :] = jnp.zeros((5, ROWS), F32)

    over(chunks, dots)
    for d in range(1, n):
        send(stats.at[me], stats.at[me], st_ss.at[d - 1], st_rs.at[d - 1], seq_to(d))

    def products(c):
        g = gbuf[rows_of(c), :]
        product[c, :root_rows, :] = dot_last(values[:root_rows, :], g)
        product[c, root_rows:, :] = dot_last(values[root_rows:, :], g)

    over(chunks, products)
    keys_t[...] = keys[...].astype(F32).T.astype(BF16)
    for d in range(1, n):
        at = seq_from(d)
        remote(stats.at[at], stats.at[at], st_ss.at[d - 1], st_rs.at[d - 1], seq_to(d)).wait_recv()

    def combine(c):
        peak = stats[0, c, 0:1, :]
        for s in range(1, n):
            peak = jnp.maximum(peak, stats[s, c, 0:1, :])
        sums, dotted = jnp.zeros((1, ROWS), F32), jnp.zeros((1, ROWS), F32)
        for s in range(n):
            factor = jnp.exp(stats[s, c, 0:1, :] - peak)
            sums = sums + stats[s, c, 1:2, :] * factor
            dotted = dotted + stats[s, c, 2:3, :] * factor
        factor = jnp.exp(stats[me, c, 0:1, :] - peak) / sums
        place[c, 1:2, :] = factor
        place[c, 2:3, :] = dotted / sums

    over(chunks, combine)

    def value_term(c, span):
        weights = probs[c, span, :] * place[c, 1:2, :]
        return dot_plain(weights.astype(BF16), gbuf[rows_of(c), :])

    def key_term(c, span):
        weights = probs[c, span, :] * place[c, 1:2, :]
        gap = product[c, span, :] - place[c, 2:3, :]
        sloped = (weights * gap).astype(BF16)
        slope[c, span, :] = sloped
        return dot_plain(sloped, qbuf[rows_of(c), :]) * scale

    def sweep(term, start, count):
        span = pl.ds(start, count)
        if chunks == 1:
            return term(0, span)
        grads[:count, :] = jnp.zeros((count, width), F32)

        def add(c):
            grads[:count, :] += term(c, span)

        over(chunks, add)
        return grads[:count, :]

    def piece_start(d):
        return pl.multiple_of(lax.rem(my_head + d, heads) * piece, 16)

    def far_pieces(at, term):
        for d in range(1, heads):
            root_part[at, d - 1] = sweep(term, piece_start(d), piece).astype(BF16)
            send(
                root_part.at[at, d - 1], root_recv.at[at, d - 1],
                rs_ss.at[at, d - 1], rs_rs.at[at, d - 1], head_to(d),
            )

    def near_piece(at, term):
        near[at] = sweep(term, piece_start(0), piece)

    def spread(at):
        term = near[at]
        for d in range(1, heads):
            remote(
                root_recv.at[at, d - 1], root_recv.at[at, d - 1],
                rs_ss.at[at, d - 1], rs_rs.at[at, d - 1], head_to(d),
            ).wait_recv()
            term = term + root_recv[at, d - 1].astype(F32)
        root_all[at, my_branch, my_head] = term.astype(BF16)
        block = root_all.at[at, my_branch, my_head]
        for d in range(1, branches):
            send(block, block, x_ss.at[at, d - 1], x_rs.at[at, d - 1], branch_to(d))
        for d in range(1, heads):
            send(block, block, hd_ss.at[at, 0, d - 1], hd_rs.at[at, 0, d - 1], head_to(d))

    far_pieces(0, value_term)
    near_piece(0, value_term)
    far_pieces(1, key_term)
    spread(0)
    near_piece(1, key_term)
    spread(1)

    for at, term in enumerate((value_term, key_term)):
        branch_all[at, my_head] = sweep(term, root_rows, branch_rows).astype(BF16)
        block = branch_all.at[at, my_head]
        for d in range(1, heads):
            send(block, block, br_ss.at[at, d - 1], br_rs.at[at, d - 1], head_to(d))

    def share_rows(buf, into, ss, rs):
        for d in range(1, n):
            far = pl.ds(pl.multiple_of(lax.rem(me + d, n) * own, 16), own)
            send(buf.at[far], into.at[d - 1], ss.at[d - 1], rs.at[d - 1], seq_to(d))

    def query_terms(c):
        term = dot_plain(keys_t[...], slope[c]) * scale
        dq_send[rows_of(c), :] = term.T.astype(BF16)

    def shares(c):
        att_send[rows_of(c), :] = (weighted[c] * place[c, 1:2, :]).T.astype(BF16)

    over(chunks, query_terms)
    share_rows(dq_send, dq_recv, dq_ss, dq_rs)
    over(chunks, shares)
    share_rows(att_send, att_recv, at_ss, at_rs)

    def forward(at):
        for d in range(1, branches):
            block = root_all.at[at, branch_from(d), my_head]
            remote(block, block, x_ss.at[at, d - 1], x_rs.at[at, d - 1], branch_to(d)).wait_recv()
            for e in range(1, heads):
                send(block, block, hd_ss.at[at, d, e - 1], hd_rs.at[at, d, e - 1], head_to(e))

    for at, out in ((0, bv_out), (1, bk_out)):
        for d in range(1, heads):
            block = branch_all.at[at, head_from(d)]
            remote(block, block, br_ss.at[at, d - 1], br_rs.at[at, d - 1], head_to(d)).wait_recv()
        term = branch_all[at, 0].astype(F32)
        for h in range(1, heads):
            term = term + branch_all[at, h].astype(F32)
        out[0] = term

    forward(0)
    forward(1)

    for at, (buf, into, ss, rs, out) in enumerate((
        (dq_send, dq_recv, dq_ss, dq_rs, dq_out), (att_send, att_recv, at_ss, at_rs, att_out)
    )):
        term = buf[mine, :].astype(F32)
        for d in range(1, n):
            remote(
                into.at[d - 1], into.at[d - 1], ss.at[d - 1], rs.at[d - 1], seq_to(d)
            ).wait_recv()
            term = term + into[d - 1].astype(F32)
        rows_f32[at] = term
        for i in range(answers):
            out[0, i] = rows_f32[at, i * per:(i + 1) * per, :].astype(out.dtype)

    for at, out in ((0, rv_out), (1, rk_out)):
        for b in range(branches):
            for d in range(1, heads):
                block = root_all.at[at, lax.rem(my_branch - b + branches, branches), head_from(d)]
                remote(
                    block, block, hd_ss.at[at, b, d - 1], hd_rs.at[at, b, d - 1], head_to(d)
                ).wait_recv()
        for h in range(heads):
            term = root_all[at, 0, h].astype(F32)
            for b in range(1, branches):
                term = term + root_all[at, b, h].astype(F32)
            out[h * piece:(h + 1) * piece, :] = term

    for copy in sends:
        copy.wait_send()


def hand_out(*refs):
    sems = refs[12]
    copies = [pltpu.make_async_copy(refs[i], refs[6 + i], sems.at[i]) for i in range(6)]
    for copy in copies:
        copy.start()
    for copy in copies:
        copy.wait()


def per_device(sizes, queries, output_cotangent, root_keys, root_values, branch_keys,
               branch_values, answer_positions):
    n, heads, branches = sizes
    answers, per, width = queries.shape[1:]
    own = answers * per
    padded = -(-n * own // ROWS) * ROWS
    chunks = padded // ROWS
    root_rows, branch_rows = root_keys.shape[0], branch_keys.shape[1]
    key_rows = root_rows + branch_rows
    piece = root_rows // heads
    vmem = pl.BlockSpec(memory_space=pltpu.VMEM)
    whole = pl.BlockSpec(memory_space=pltpu.HBM)

    def sem(*shape):
        return pltpu.SemaphoreType.DMA(tuple(max(1, size) for size in shape))

    z, h, b = max(1, n - 1), max(1, heads - 1), max(1, branches - 1)
    scratch = [
        pltpu.VMEM(answer_positions.shape, jnp.int32),
        pltpu.VMEM((key_rows, width), BF16),
        pltpu.VMEM((key_rows, width), BF16),
        pltpu.VMEM((width, key_rows), BF16),
        pltpu.VMEM((width, key_rows), BF16),
        pltpu.VMEM((2, own, width), F32),
        pltpu.VMEM((padded, width), BF16),
        pltpu.VMEM((padded, width), BF16),
        pltpu.VMEM((n, chunks, 8, ROWS), F32),
        pltpu.VMEM((chunks, key_rows, ROWS), F32),
        pltpu.VMEM((chunks, key_rows, ROWS), F32),
        pltpu.VMEM((chunks, width, ROWS), F32),
        pltpu.VMEM((chunks, 8, ROWS), F32),
        pltpu.VMEM((padded, width), BF16),
        pltpu.VMEM((z, own, width), BF16),
        pltpu.VMEM((2, piece, width), F32),
        pltpu.VMEM((padded, width), BF16),
        pltpu.VMEM((z, own, width), BF16),
        pltpu.VMEM((2, h, piece, width), BF16),
        pltpu.VMEM((2, h, piece, width), BF16),
        pltpu.VMEM((2, branches, heads, piece, width), BF16),
        pltpu.VMEM((2, heads, branch_rows, width), BF16),
        pltpu.VMEM((chunks, key_rows, ROWS), BF16),
        pltpu.VMEM((max(root_rows, branch_rows), width), F32),
        sem(7),
        sem(z), sem(z), sem(z), sem(z), sem(z), sem(z), sem(z), sem(z), sem(z), sem(z),
        sem(2, h), sem(2, h), sem(2, b), sem(2, b),
        sem(2, branches, h), sem(2, branches, h), sem(2, h), sem(2, h),
    ]
    outs = (
        jax.ShapeDtypeStruct(queries.shape, BF16),
        jax.ShapeDtypeStruct(queries.shape, F32),
        jax.ShapeDtypeStruct(root_keys.shape, F32),
        jax.ShapeDtypeStruct(root_values.shape, F32),
        jax.ShapeDtypeStruct(branch_keys.shape, F32),
        jax.ShapeDtypeStruct(branch_values.shape, F32),
    )
    results = pl.pallas_call(
        functools.partial(kernel, sizes),
        out_shape=outs,
        in_specs=[whole] * 7,
        out_specs=[vmem] * 6,
        scratch_shapes=scratch,
        compiler_params=pltpu.CompilerParams(
            collective_id=0, has_side_effects=True, vmem_limit_bytes=48 * 1024 * 1024
        ),
    )(*(
        pltpu.with_memory_space_constraint(array, pltpu.HBM) for array in (
            queries.reshape(own, width), output_cotangent.reshape(own, width),
            answer_positions, root_keys, root_values,
            branch_keys, branch_values,
        )
    ))
    return pl.pallas_call(
        hand_out,
        out_shape=outs,
        in_specs=[vmem] * 6,
        out_specs=[whole] * 6,
        scratch_shapes=[pltpu.SemaphoreType.DMA((6,))],
        compiler_params=pltpu.CompilerParams(vmem_limit_bytes=2 * 1024 * 1024),
    )(*results)


def solution(mesh):
    sizes = (mesh.shape["seq"], mesh.shape["head"], mesh.shape["branch"])
    rows = P(("parts", "branch"), "seq", "head", None)
    root = P(("parts", "seq"), None)
    branch = P(("parts", "branch"), "seq", None)
    return jax.shard_map(
        functools.partial(per_device, sizes),
        mesh=mesh,
        in_specs=(rows, rows, root, root, branch, branch, P(("parts", "branch"), None)),
        out_specs=(rows, rows, root, root, branch, branch),
        check_vma=False,
    )
```

```python
import functools
import math

import jax
import jax.numpy as jnp
from jax import lax
from jax.experimental import pallas as pl
from jax.experimental.pallas import tpu as pltpu
from jax.sharding import PartitionSpec as P

NEG = -1e30
ROWS = 256
F32 = jnp.float32
BF16 = jnp.bfloat16


def dot_last(left, right):
    return lax.dot_general(left, right, (((1,), (1,)), ((), ())), preferred_element_type=F32)


def dot_plain(left, right):
    return jnp.dot(left, right, preferred_element_type=F32)


def remote(src, dst, send, recv, device):
    return pltpu.make_async_remote_copy(
        src_ref=src,
        dst_ref=dst,
        send_sem=send,
        recv_sem=recv,
        device_id=device,
        device_id_type=pl.DeviceIdType.MESH,
    )


def over(count, body):
    if count == 1:
        body(0)
    else:
        lax.fori_loop(0, count, lambda at, carry: (body(at), carry)[1], 0)


def kernel(
    sizes,
    q_hbm, g_hbm, pos_hbm, rk_hbm, rv_hbm, bk_hbm, bv_hbm,
    att_out, dq_out, rk_out, rv_out, bk_out, bv_out,
    pos_ref, keys, values, keys_t, values_t, rows_f32, qbuf, gbuf, stats, probs, product, weighted, place,
    att_send, att_recv, dq_send, dq_recv,
    q_far, g_far, place_far, terms, root_all, branch_all, slope, grads,
    load_sem, q_ss, q_rs, g_ss, g_rs, st_ss, st_rs, at_ss, at_rs, dq_ss, dq_rs,
    rs_ss, rs_rs, x_ss, x_rs, xq_ss, xq_rs, xg_ss, xg_rs, br_ss, br_rs,
):
    n, heads, branches = sizes
    me, my_head, my_branch = (
        lax.axis_index("seq"), lax.axis_index("head"), lax.axis_index("branch")
    )
    own, width = q_hbm.shape
    answers, per = att_out.shape[1:3]
    padded = qbuf.shape[0]
    chunks = padded // ROWS
    root_rows, branch_rows = rk_hbm.shape[0], bk_hbm.shape[1]
    scale = 1.0 / math.sqrt(width)

    def seq_to(d):
        return {"seq": lax.rem(me + d, n)}

    def seq_from(d):
        return lax.rem(me - d + n, n)

    def head_to(d):
        return {"head": lax.rem(my_head + d, heads)}

    def head_from(d):
        return lax.rem(my_head - d + heads, heads)

    def branch_to(d):
        return {"branch": lax.rem(my_branch + d, branches)}

    def branch_from(d):
        return lax.rem(my_branch - d + branches, branches)

    barrier = pltpu.get_barrier_semaphore()
    for to, count in ((seq_to, n), (head_to, heads), (branch_to, branches)):
        for d in range(1, count):
            pl.semaphore_signal(
                barrier, inc=1, device_id=to(d), device_id_type=pl.DeviceIdType.MESH
            )

    mine = pl.ds(pl.multiple_of(me * own, 16), own)
    loads = [
        pltpu.make_async_copy(q_hbm, qbuf.at[mine], load_sem.at[4]),
        pltpu.make_async_copy(g_hbm, gbuf.at[mine], load_sem.at[5]),
        pltpu.make_async_copy(pos_hbm, pos_ref, load_sem.at[6]),
        pltpu.make_async_copy(rk_hbm, keys.at[pl.ds(0, root_rows)], load_sem.at[0]),
        pltpu.make_async_copy(bk_hbm.at[0], keys.at[pl.ds(root_rows, branch_rows)], load_sem.at[1]),
        pltpu.make_async_copy(rv_hbm, values.at[pl.ds(0, root_rows)], load_sem.at[2]),
        pltpu.make_async_copy(bv_hbm.at[0], values.at[pl.ds(root_rows, branch_rows)], load_sem.at[3]),
    ]
    for load in loads:
        load.start()

    pl.semaphore_wait(barrier, (n - 1) + (heads - 1) + (branches - 1))

    sends = []

    def send(*pieces):
        copy = remote(*pieces)
        copy.start()
        sends.append(copy)

    for load, buf, ss, rs in ((loads[0], qbuf, q_ss, q_rs), (loads[1], gbuf, g_ss, g_rs)):
        load.wait()
        for d in range(1, n):
            send(buf.at[mine], buf.at[mine], ss.at[d - 1], rs.at[d - 1], seq_to(d))

    def across(buf, far, ss, rs, d):
        rows = pl.ds(pl.multiple_of(seq_from(d) * own, 16), own)
        for e in range(1, branches):
            send(buf.at[rows], far.at[e - 1, rows], ss.at[e - 1, d], rs.at[e - 1, d], branch_to(e))

    across(qbuf, q_far, xq_ss, xq_rs, 0)
    across(gbuf, g_far, xg_ss, xg_rs, 0)

    if padded > n * own:
        for target in (qbuf, gbuf):
            target[n * own:, :] = jnp.zeros((padded - n * own, width), BF16)
        for target in (q_far, g_far):
            for e in range(1, branches):
                target[e - 1, n * own:, :] = jnp.zeros((padded - n * own, width), BF16)

    def arrived_rows(buf, ss, rs, far, far_ss, far_rs):
        for d in range(1, n):
            rows = pl.ds(pl.multiple_of(seq_from(d) * own, 16), own)
            remote(buf.at[rows], buf.at[rows], ss.at[d - 1], rs.at[d - 1], seq_to(d)).wait_recv()
            across(buf, far, far_ss, far_rs, d)

    loads[2].wait()
    total = pos_ref.shape[1]
    spot = jnp.broadcast_to(pos_ref[...], (8, total))
    high = (spot >> 7).astype(F32).astype(BF16)
    low = (spot & 127).astype(F32).astype(BF16)

    def expand(c):
        row = lax.broadcasted_iota(jnp.int32, (total, ROWS), 1) + c * ROWS
        answer = lax.broadcasted_iota(jnp.int32, (total, ROWS), 0)
        pick = (row >= answer * per) & (row < answer * per + per)
        pick = jnp.where(pick, 1.0, 0.0).astype(BF16)
        place[c] = dot_plain(high, pick) * 128.0 + dot_plain(low, pick)

    over(chunks, expand)

    for load in loads[3:]:
        load.wait()
    values_t[...] = values[...].astype(F32).T.astype(BF16)
    arrived_rows(qbuf, q_ss, q_rs, q_far, xq_ss, xq_rs)

    key_place = (
        lax.broadcasted_iota(jnp.int32, (branch_rows, ROWS), 0) + me * branch_rows
    ).astype(F32)

    def rows_of(c):
        return pl.ds(c * ROWS if isinstance(c, int) else pl.multiple_of(c * ROWS, ROWS), ROWS)

    def scores(c):
        q = qbuf[rows_of(c), :]
        on_root = dot_last(keys[:root_rows, :], q) * scale
        on_branch = dot_last(keys[root_rows:, :], q) * scale
        on_branch = jnp.where(key_place <= place[c, 0:1, :], on_branch, NEG)
        peak = jnp.maximum(
            jnp.max(on_root, axis=0, keepdims=True), jnp.max(on_branch, axis=0, keepdims=True)
        )
        p_root = jnp.exp(on_root - peak)
        p_branch = jnp.exp(on_branch - peak)
        probs[c, :root_rows, :] = on_root
        probs[c, root_rows:, :] = p_branch
        sums = jnp.sum(p_root, axis=0, keepdims=True) + jnp.sum(p_branch, axis=0, keepdims=True)
        share = dot_plain(values_t[:, :root_rows], p_root.astype(BF16))
        share = share + dot_plain(values_t[:, root_rows:], p_branch.astype(BF16))
        weighted[c] = share
        stats[me, c, 0:1, :] = peak
        stats[me, c, 1:2, :] = sums

    over(chunks, scores)
    arrived_rows(gbuf, g_ss, g_rs, g_far, xg_ss, xg_rs)

    def dots(c):
        turned = gbuf[rows_of(c), :].astype(F32).T
        stats[me, c, 2:3, :] = jnp.sum(weighted[c] * turned, axis=0, keepdims=True)
        stats[me, c, 3:8, :] = jnp.zeros((5, ROWS), F32)

    over(chunks, dots)
    for d in range(1, n):
        send(stats.at[me], stats.at[me], st_ss.at[d - 1], st_rs.at[d - 1], seq_to(d))

    def products(c):
        g = gbuf[rows_of(c), :]
        product[c, :root_rows, :] = dot_last(values[:root_rows, :], g)
        product[c, root_rows:, :] = dot_last(values[root_rows:, :], g)

    over(chunks, products)
    keys_t[...] = keys[...].astype(F32).T.astype(BF16)
    for d in range(1, n):
        at = seq_from(d)
        remote(stats.at[at], stats.at[at], st_ss.at[d - 1], st_rs.at[d - 1], seq_to(d)).wait_recv()

    def combine(c):
        peak = stats[0, c, 0:1, :]
        for s in range(1, n):
            peak = jnp.maximum(peak, stats[s, c, 0:1, :])
        sums, dotted = jnp.zeros((1, ROWS), F32), jnp.zeros((1, ROWS), F32)
        for s in range(n):
            factor = jnp.exp(stats[s, c, 0:1, :] - peak)
            sums = sums + stats[s, c, 1:2, :] * factor
            dotted = dotted + stats[s, c, 2:3, :] * factor
        factor = jnp.exp(stats[me, c, 0:1, :] - peak) / sums
        place[c, 1:2, :] = factor
        place[c, 2:3, :] = dotted / sums
        place[c, 3:4, :] = peak
        place[c, 4:5, :] = 1.0 / sums

    over(chunks, combine)

    for e in range(1, branches):
        send(place, place_far.at[e - 1], x_ss.at[e - 1], x_rs.at[e - 1], branch_to(e))

    def root_weights(score, norm):
        return jnp.exp(score - norm[3:4, :]) * norm[4:5, :]

    def root_value_term(score, norm, g):
        return dot_plain(root_weights(score, norm).astype(BF16), g)

    def root_key_term(score, gap, norm, q):
        sloped = (root_weights(score, norm) * (gap - norm[2:3, :])).astype(BF16)
        return sloped, dot_plain(sloped, q) * scale

    def put(at, branch, c, term):
        if chunks == 1:
            terms[at, branch] = term
            return
        kept = jnp.where(c == 0, 0.0, terms[at, branch])
        terms[at, branch] = kept + term

    def own_root(c):
        score, norm = probs[c, :root_rows, :], place[c]
        put(0, my_branch, c, root_value_term(score, norm, gbuf[rows_of(c), :]))
        sloped, term = root_key_term(score, product[c, :root_rows, :], norm, qbuf[rows_of(c), :])
        slope[c, :root_rows, :] = sloped
        put(1, my_branch, c, term)

    def branch_value_term(c):
        weights = probs[c, root_rows:, :] * place[c, 1:2, :]
        return dot_plain(weights.astype(BF16), gbuf[rows_of(c), :])

    def branch_key_term(c):
        weights = probs[c, root_rows:, :] * place[c, 1:2, :]
        gap = product[c, root_rows:, :] - place[c, 2:3, :]
        sloped = (weights * gap).astype(BF16)
        slope[c, root_rows:, :] = sloped
        return dot_plain(sloped, qbuf[rows_of(c), :]) * scale

    def sweep(term, count):
        if chunks == 1:
            return term(0)
        grads[:count, :] = jnp.zeros((count, width), F32)

        def add(c):
            grads[:count, :] += term(c)

        over(chunks, add)
        return grads[:count, :]

    def to_heads(buf, at, term, ss, rs):
        buf[at, my_head] = term.astype(BF16)
        block = buf.at[at, my_head]
        for d in range(1, heads):
            send(block, block, ss.at[at, d - 1], rs.at[at, d - 1], head_to(d))

    def from_heads(buf, at, ss, rs):
        for d in range(1, heads):
            block = buf.at[at, head_from(d)]
            remote(block, block, ss.at[at, d - 1], rs.at[at, d - 1], head_to(d)).wait_recv()
        term = buf[at, 0].astype(F32)
        for h in range(1, heads):
            term = term + buf[at, h].astype(F32)
        return term

    over(chunks, own_root)
    for at, term in enumerate((branch_value_term, branch_key_term)):
        to_heads(branch_all, at, sweep(term, branch_rows), br_ss, br_rs)

    def share_rows(buf, into, ss, rs):
        for d in range(1, n):
            far = pl.ds(pl.multiple_of(lax.rem(me + d, n) * own, 16), own)
            send(buf.at[far], into.at[d - 1], ss.at[d - 1], rs.at[d - 1], seq_to(d))

    def query_terms(c):
        term = dot_plain(keys_t[...], slope[c]) * scale
        dq_send[rows_of(c), :] = term.T.astype(BF16)

    def shares(c):
        att_send[rows_of(c), :] = (weighted[c] * place[c, 1:2, :]).T.astype(BF16)

    over(chunks, query_terms)
    share_rows(dq_send, dq_recv, dq_ss, dq_rs)
    over(chunks, shares)
    share_rows(att_send, att_recv, at_ss, at_rs)

    for e in range(1, branches):
        for far, ss, rs in ((q_far, xq_ss, xq_rs), (g_far, xg_ss, xg_rs)):
            for d in range(n):
                rows = far.at[e - 1, pl.ds(pl.multiple_of(seq_from(d) * own, 16), own)]
                remote(rows, rows, ss.at[e - 1, d], rs.at[e - 1, d], branch_to(e)).wait_recv()
        norms = place_far.at[e - 1]
        remote(norms, norms, x_ss.at[e - 1], x_rs.at[e - 1], branch_to(e)).wait_recv()

    def far_score(e, c):
        return dot_last(keys[:root_rows, :], q_far[e - 1, rows_of(c), :]) * scale

    def far_values(e, c):
        term = root_value_term(far_score(e, c), place_far[e - 1, c], g_far[e - 1, rows_of(c), :])
        put(0, branch_from(e), c, term)

    def far_keys(e, c):
        gap = dot_last(values[:root_rows, :], g_far[e - 1, rows_of(c), :])
        q = q_far[e - 1, rows_of(c), :]
        put(1, branch_from(e), c, root_key_term(far_score(e, c), gap, place_far[e - 1, c], q)[1])

    for at, far in enumerate((far_values, far_keys)):
        for e in range(1, branches):
            over(chunks, functools.partial(far, e))
        term = terms[at, 0]
        for b in range(1, branches):
            term = term + terms[at, b]
        to_heads(root_all, at, term, rs_ss, rs_rs)

    bv_out[0] = from_heads(branch_all, 0, br_ss, br_rs)
    bk_out[0] = from_heads(branch_all, 1, br_ss, br_rs)

    for at, (buf, into, ss, rs, out) in enumerate((
        (dq_send, dq_recv, dq_ss, dq_rs, dq_out), (att_send, att_recv, at_ss, at_rs, att_out)
    )):
        term = buf[mine, :].astype(F32)
        for d in range(1, n):
            remote(
                into.at[d - 1], into.at[d - 1], ss.at[d - 1], rs.at[d - 1], seq_to(d)
            ).wait_recv()
            term = term + into[d - 1].astype(F32)
        rows_f32[at] = term
        for i in range(answers):
            out[0, i] = rows_f32[at, i * per:(i + 1) * per, :].astype(out.dtype)

    rv_out[...] = from_heads(root_all, 0, rs_ss, rs_rs)
    rk_out[...] = from_heads(root_all, 1, rs_ss, rs_rs)

    for copy in sends:
        copy.wait_send()


def hand_out(*refs):
    sems = refs[12]
    copies = [pltpu.make_async_copy(refs[i], refs[6 + i], sems.at[i]) for i in range(6)]
    for copy in copies:
        copy.start()
    for copy in copies:
        copy.wait()


def per_device(sizes, queries, output_cotangent, root_keys, root_values, branch_keys,
               branch_values, answer_positions):
    n, heads, branches = sizes
    answers, per, width = queries.shape[1:]
    own = answers * per
    padded = -(-n * own // ROWS) * ROWS
    chunks = padded // ROWS
    root_rows, branch_rows = root_keys.shape[0], branch_keys.shape[1]
    key_rows = root_rows + branch_rows
    vmem = pl.BlockSpec(memory_space=pltpu.VMEM)
    whole = pl.BlockSpec(memory_space=pltpu.HBM)

    def sem(*shape):
        return pltpu.SemaphoreType.DMA(tuple(max(1, size) for size in shape))

    z, h, b = max(1, n - 1), max(1, heads - 1), max(1, branches - 1)
    scratch = [
        pltpu.VMEM(answer_positions.shape, jnp.int32),
        pltpu.VMEM((key_rows, width), BF16),
        pltpu.VMEM((key_rows, width), BF16),
        pltpu.VMEM((width, key_rows), BF16),
        pltpu.VMEM((width, key_rows), BF16),
        pltpu.VMEM((2, own, width), F32),
        pltpu.VMEM((padded, width), BF16),
        pltpu.VMEM((padded, width), BF16),
        pltpu.VMEM((n, chunks, 8, ROWS), F32),
        pltpu.VMEM((chunks, key_rows, ROWS), F32),
        pltpu.VMEM((chunks, key_rows, ROWS), F32),
        pltpu.VMEM((chunks, width, ROWS), F32),
        pltpu.VMEM((chunks, 8, ROWS), F32),
        pltpu.VMEM((padded, width), BF16),
        pltpu.VMEM((z, own, width), BF16),
        pltpu.VMEM((padded, width), BF16),
        pltpu.VMEM((z, own, width), BF16),
        pltpu.VMEM((b, padded, width), BF16),
        pltpu.VMEM((b, padded, width), BF16),
        pltpu.VMEM((b, chunks, 8, ROWS), F32),
        pltpu.VMEM((2, branches, root_rows, width), F32),
        pltpu.VMEM((2, heads, root_rows, width), BF16),
        pltpu.VMEM((2, heads, branch_rows, width), BF16),
        pltpu.VMEM((chunks, key_rows, ROWS), BF16),
        pltpu.VMEM((branch_rows, width), F32),
        sem(7),
        sem(z), sem(z), sem(z), sem(z), sem(z), sem(z), sem(z), sem(z), sem(z), sem(z),
        sem(2, h), sem(2, h), sem(b), sem(b),
        sem(b, n), sem(b, n), sem(b, n), sem(b, n), sem(2, h), sem(2, h),
    ]
    outs = (
        jax.ShapeDtypeStruct(queries.shape, BF16),
        jax.ShapeDtypeStruct(queries.shape, F32),
        jax.ShapeDtypeStruct(root_keys.shape, F32),
        jax.ShapeDtypeStruct(root_values.shape, F32),
        jax.ShapeDtypeStruct(branch_keys.shape, F32),
        jax.ShapeDtypeStruct(branch_values.shape, F32),
    )
    results = pl.pallas_call(
        functools.partial(kernel, sizes),
        out_shape=outs,
        in_specs=[whole] * 7,
        out_specs=[vmem] * 6,
        scratch_shapes=scratch,
        compiler_params=pltpu.CompilerParams(
            collective_id=0, has_side_effects=True, vmem_limit_bytes=48 * 1024 * 1024
        ),
    )(*(
        pltpu.with_memory_space_constraint(array, pltpu.HBM) for array in (
            queries.reshape(own, width), output_cotangent.reshape(own, width),
            answer_positions, root_keys, root_values,
            branch_keys, branch_values,
        )
    ))
    return pl.pallas_call(
        hand_out,
        out_shape=outs,
        in_specs=[vmem] * 6,
        out_specs=[whole] * 6,
        scratch_shapes=[pltpu.SemaphoreType.DMA((6,))],
        compiler_params=pltpu.CompilerParams(vmem_limit_bytes=2 * 1024 * 1024),
    )(*results)


def solution(mesh):
    sizes = (mesh.shape["seq"], mesh.shape["head"], mesh.shape["branch"])
    rows = P(("parts", "branch"), "seq", "head", None)
    root = P(("parts", "seq"), None)
    branch = P(("parts", "branch"), "seq", None)
    return jax.shard_map(
        functools.partial(per_device, sizes),
        mesh=mesh,
        in_specs=(rows, rows, root, root, branch, branch, P(("parts", "branch"), None)),
        out_specs=(rows, rows, root, root, branch, branch),
        check_vma=False,
    )
```

```python
import functools
import math

import jax
import jax.numpy as jnp
from jax import lax
from jax.experimental import pallas as pl
from jax.experimental.pallas import tpu as pltpu
from jax.sharding import PartitionSpec as P

NEG = -1e30
ROWS = 256
F32 = jnp.float32
BF16 = jnp.bfloat16


def dot_last(left, right):
    return lax.dot_general(left, right, (((1,), (1,)), ((), ())), preferred_element_type=F32)


def dot_plain(left, right):
    return jnp.dot(left, right, preferred_element_type=F32)


def remote(src, dst, send, recv, device):
    return pltpu.make_async_remote_copy(
        src_ref=src,
        dst_ref=dst,
        send_sem=send,
        recv_sem=recv,
        device_id=device,
        device_id_type=pl.DeviceIdType.MESH,
    )


def over(count, body):
    if count == 1:
        body(0)
    else:
        lax.fori_loop(0, count, lambda at, carry: (body(at), carry)[1], 0)


def kernel(
    sizes,
    q_hbm, g_hbm, pos_hbm, rk_hbm, rv_hbm, bk_hbm, bv_hbm,
    att_out, dq_out, rk_out, rv_out, bk_out, bv_out,
    pos_ref, keys, values, keys_t, values_t, rows_f32, qbuf, gbuf, stats, probs, product, weighted, place,
    att_send, att_recv, dq_send, dq_recv,
    q_far, g_far, score_far, place_far, terms, root_all, branch_all, slope, grads,
    load_sem, q_ss, q_rs, g_ss, g_rs, st_ss, st_rs, at_ss, at_rs, dq_ss, dq_rs,
    rs_ss, rs_rs, x_ss, x_rs, xq_ss, xq_rs, xg_ss, xg_rs, br_ss, br_rs,
):
    n, heads, branches = sizes
    me, my_head, my_branch = (
        lax.axis_index("seq"), lax.axis_index("head"), lax.axis_index("branch")
    )
    own, width = q_hbm.shape
    answers, per = att_out.shape[1:3]
    padded = qbuf.shape[0]
    chunks = padded // ROWS
    root_rows, branch_rows = rk_hbm.shape[0], bk_hbm.shape[1]
    scale = 1.0 / math.sqrt(width)

    def seq_to(d):
        return {"seq": lax.rem(me + d, n)}

    def seq_from(d):
        return lax.rem(me - d + n, n)

    def head_to(d):
        return {"head": lax.rem(my_head + d, heads)}

    def head_from(d):
        return lax.rem(my_head - d + heads, heads)

    def branch_to(d):
        return {"branch": lax.rem(my_branch + d, branches)}

    def branch_from(d):
        return lax.rem(my_branch - d + branches, branches)

    barrier = pltpu.get_barrier_semaphore()
    for to, count in ((seq_to, n), (head_to, heads), (branch_to, branches)):
        for d in range(1, count):
            pl.semaphore_signal(
                barrier, inc=1, device_id=to(d), device_id_type=pl.DeviceIdType.MESH
            )

    mine = pl.ds(pl.multiple_of(me * own, 16), own)
    loads = [
        pltpu.make_async_copy(q_hbm, qbuf.at[mine], load_sem.at[4]),
        pltpu.make_async_copy(g_hbm, gbuf.at[mine], load_sem.at[5]),
        pltpu.make_async_copy(pos_hbm, pos_ref, load_sem.at[6]),
        pltpu.make_async_copy(rk_hbm, keys.at[pl.ds(0, root_rows)], load_sem.at[0]),
        pltpu.make_async_copy(bk_hbm.at[0], keys.at[pl.ds(root_rows, branch_rows)], load_sem.at[1]),
        pltpu.make_async_copy(rv_hbm, values.at[pl.ds(0, root_rows)], load_sem.at[2]),
        pltpu.make_async_copy(bv_hbm.at[0], values.at[pl.ds(root_rows, branch_rows)], load_sem.at[3]),
    ]
    for load in loads:
        load.start()

    pl.semaphore_wait(barrier, (n - 1) + (heads - 1) + (branches - 1))

    sends = []

    def send(*pieces):
        copy = remote(*pieces)
        copy.start()
        sends.append(copy)

    for source, buf, ss, rs in ((q_hbm, qbuf, q_ss, q_rs), (g_hbm, gbuf, g_ss, g_rs)):
        for d in range(1, n):
            send(source, buf.at[mine], ss.at[d - 1], rs.at[d - 1], seq_to(d))

    def across(buf, far, ss, rs, d):
        rows = pl.ds(pl.multiple_of(seq_from(d) * own, 16), own)
        source = buf if d == 0 else buf.at[rows]
        for e in range(1, branches):
            send(source, far.at[e - 1, rows], ss.at[e - 1, d], rs.at[e - 1, d], branch_to(e))

    across(q_hbm, q_far, xq_ss, xq_rs, 0)
    across(g_hbm, g_far, xg_ss, xg_rs, 0)

    if padded > n * own:
        for target in (qbuf, gbuf):
            target[n * own:, :] = jnp.zeros((padded - n * own, width), BF16)
        for target in (q_far, g_far):
            for e in range(1, branches):
                target[e - 1, n * own:, :] = jnp.zeros((padded - n * own, width), BF16)

    def arrived_rows(buf, ss, rs, far, far_ss, far_rs):
        for d in range(1, n):
            rows = pl.ds(pl.multiple_of(seq_from(d) * own, 16), own)
            remote(buf.at[rows], buf.at[rows], ss.at[d - 1], rs.at[d - 1], seq_to(d)).wait_recv()
            across(buf, far, far_ss, far_rs, d)

    loads[2].wait()
    total = pos_ref.shape[1]
    spot = jnp.broadcast_to(pos_ref[...], (8, total))
    high = (spot >> 7).astype(F32).astype(BF16)
    low = (spot & 127).astype(F32).astype(BF16)

    def expand(c):
        row = lax.broadcasted_iota(jnp.int32, (total, ROWS), 1) + c * ROWS
        answer = lax.broadcasted_iota(jnp.int32, (total, ROWS), 0)
        pick = (row >= answer * per) & (row < answer * per + per)
        pick = jnp.where(pick, 1.0, 0.0).astype(BF16)
        place[c] = dot_plain(high, pick) * 128.0 + dot_plain(low, pick)

    over(chunks, expand)

    for load in loads[:2] + loads[3:]:
        load.wait()
    values_t[...] = values[...].astype(F32).T.astype(BF16)
    arrived_rows(qbuf, q_ss, q_rs, q_far, xq_ss, xq_rs)

    key_place = (
        lax.broadcasted_iota(jnp.int32, (branch_rows, ROWS), 0) + me * branch_rows
    ).astype(F32)

    def rows_of(c):
        return pl.ds(c * ROWS if isinstance(c, int) else pl.multiple_of(c * ROWS, ROWS), ROWS)

    def scores(c):
        q = qbuf[rows_of(c), :]
        on_root = dot_last(keys[:root_rows, :], q) * scale
        on_branch = dot_last(keys[root_rows:, :], q) * scale
        on_branch = jnp.where(key_place <= place[c, 0:1, :], on_branch, NEG)
        peak = jnp.maximum(
            jnp.max(on_root, axis=0, keepdims=True), jnp.max(on_branch, axis=0, keepdims=True)
        )
        p_root = jnp.exp(on_root - peak)
        p_branch = jnp.exp(on_branch - peak)
        probs[c, :root_rows, :] = on_root
        probs[c, root_rows:, :] = p_branch
        sums = jnp.sum(p_root, axis=0, keepdims=True) + jnp.sum(p_branch, axis=0, keepdims=True)
        slope[c, :root_rows, :] = p_root.astype(BF16)
        slope[c, root_rows:, :] = p_branch.astype(BF16)
        stats[me, c, 0:1, :] = peak
        stats[me, c, 1:2, :] = sums

    over(chunks, scores)
    arrived_rows(gbuf, g_ss, g_rs, g_far, xg_ss, xg_rs)

    def dots(c):
        turned = gbuf[rows_of(c), :].astype(F32).T
        share = dot_plain(values_t[...], slope[c])
        weighted[c] = share
        stats[me, c, 2:3, :] = jnp.sum(share * turned, axis=0, keepdims=True)
        stats[me, c, 3:8, :] = jnp.zeros((5, ROWS), F32)

    over(chunks, dots)
    for d in range(1, n):
        send(stats.at[me], stats.at[me], st_ss.at[d - 1], st_rs.at[d - 1], seq_to(d))

    def products(c):
        g = gbuf[rows_of(c), :]
        product[c, :root_rows, :] = dot_last(values[:root_rows, :], g)
        product[c, root_rows:, :] = dot_last(values[root_rows:, :], g)

    over(chunks, products)
    keys_t[...] = keys[...].astype(F32).T.astype(BF16)

    def arrived_far(far, ss, rs):
        for e in range(1, branches):
            for d in range(n):
                rows = far.at[e - 1, pl.ds(pl.multiple_of(seq_from(d) * own, 16), own)]
                remote(rows, rows, ss.at[e - 1, d], rs.at[e - 1, d], branch_to(e)).wait_recv()

    arrived_far(q_far, xq_ss, xq_rs)
    for e in range(1, branches):

        def far_scores(c, e=e):
            q = q_far[e - 1, rows_of(c), :]
            score_far[e - 1, c] = dot_last(keys[:root_rows, :], q) * scale

        over(chunks, far_scores)

    for d in range(1, n):
        at = seq_from(d)
        remote(stats.at[at], stats.at[at], st_ss.at[d - 1], st_rs.at[d - 1], seq_to(d)).wait_recv()

    def combine(c):
        peak = stats[0, c, 0:1, :]
        for s in range(1, n):
            peak = jnp.maximum(peak, stats[s, c, 0:1, :])
        sums, dotted = jnp.zeros((1, ROWS), F32), jnp.zeros((1, ROWS), F32)
        for s in range(n):
            factor = jnp.exp(stats[s, c, 0:1, :] - peak)
            sums = sums + stats[s, c, 1:2, :] * factor
            dotted = dotted + stats[s, c, 2:3, :] * factor
        factor = jnp.exp(stats[me, c, 0:1, :] - peak) / sums
        place[c, 1:2, :] = factor
        place[c, 2:3, :] = dotted / sums
        place[c, 3:4, :] = peak
        place[c, 4:5, :] = 1.0 / sums

    over(chunks, combine)

    for e in range(1, branches):
        send(place, place_far.at[e - 1], x_ss.at[e - 1], x_rs.at[e - 1], branch_to(e))

    def root_weights(score, norm):
        return jnp.exp(score - norm[3:4, :]) * norm[4:5, :]

    def root_value_term(score, norm, g):
        return dot_plain(root_weights(score, norm).astype(BF16), g)

    def root_key_term(score, gap, norm, q):
        sloped = (root_weights(score, norm) * (gap - norm[2:3, :])).astype(BF16)
        return sloped, dot_plain(sloped, q) * scale

    def put(at, branch, c, term):
        if chunks == 1:
            terms[at, branch] = term
            return
        kept = jnp.where(c == 0, 0.0, terms[at, branch])
        terms[at, branch] = kept + term

    def own_root(c):
        score, norm = probs[c, :root_rows, :], place[c]
        put(0, my_branch, c, root_value_term(score, norm, gbuf[rows_of(c), :]))
        sloped, term = root_key_term(score, product[c, :root_rows, :], norm, qbuf[rows_of(c), :])
        slope[c, :root_rows, :] = sloped
        put(1, my_branch, c, term)

    def branch_value_term(c):
        weights = probs[c, root_rows:, :] * place[c, 1:2, :]
        return dot_plain(weights.astype(BF16), gbuf[rows_of(c), :])

    def branch_key_term(c):
        weights = probs[c, root_rows:, :] * place[c, 1:2, :]
        gap = product[c, root_rows:, :] - place[c, 2:3, :]
        sloped = (weights * gap).astype(BF16)
        slope[c, root_rows:, :] = sloped
        return dot_plain(sloped, qbuf[rows_of(c), :]) * scale

    def sweep(term, count):
        if chunks == 1:
            return term(0)
        grads[:count, :] = jnp.zeros((count, width), F32)

        def add(c):
            grads[:count, :] += term(c)

        over(chunks, add)
        return grads[:count, :]

    def to_heads(buf, at, term, ss, rs):
        buf[at, my_head] = term.astype(BF16)
        block = buf.at[at, my_head]
        for d in range(1, heads):
            send(block, block, ss.at[at, d - 1], rs.at[at, d - 1], head_to(d))

    def from_heads(buf, at, ss, rs):
        for d in range(1, heads):
            block = buf.at[at, head_from(d)]
            remote(block, block, ss.at[at, d - 1], rs.at[at, d - 1], head_to(d)).wait_recv()
        term = buf[at, 0].astype(F32)
        for h in range(1, heads):
            term = term + buf[at, h].astype(F32)
        return term

    over(chunks, own_root)
    for at, term in enumerate((branch_value_term, branch_key_term)):
        to_heads(branch_all, at, sweep(term, branch_rows), br_ss, br_rs)

    def share_rows(buf, into, ss, rs):
        for d in range(1, n):
            far = pl.ds(pl.multiple_of(lax.rem(me + d, n) * own, 16), own)
            send(buf.at[far], into.at[d - 1], ss.at[d - 1], rs.at[d - 1], seq_to(d))

    def query_terms(c):
        term = dot_plain(keys_t[...], slope[c]) * scale
        dq_send[rows_of(c), :] = term.T.astype(BF16)

    def shares(c):
        att_send[rows_of(c), :] = (weighted[c] * place[c, 1:2, :]).T.astype(BF16)

    over(chunks, query_terms)
    share_rows(dq_send, dq_recv, dq_ss, dq_rs)
    over(chunks, shares)
    share_rows(att_send, att_recv, at_ss, at_rs)

    arrived_far(g_far, xg_ss, xg_rs)
    for e in range(1, branches):
        norms = place_far.at[e - 1]
        remote(norms, norms, x_ss.at[e - 1], x_rs.at[e - 1], branch_to(e)).wait_recv()

    def far_values(e, c):
        term = root_value_term(score_far[e - 1, c], place_far[e - 1, c], g_far[e - 1, rows_of(c), :])
        put(0, branch_from(e), c, term)

    def far_keys(e, c):
        gap = dot_last(values[:root_rows, :], g_far[e - 1, rows_of(c), :])
        q = q_far[e - 1, rows_of(c), :]
        put(1, branch_from(e), c, root_key_term(score_far[e - 1, c], gap, place_far[e - 1, c], q)[1])

    for at, far in enumerate((far_values, far_keys)):
        for e in range(1, branches):
            over(chunks, functools.partial(far, e))
        term = terms[at, 0]
        for b in range(1, branches):
            term = term + terms[at, b]
        to_heads(root_all, at, term, rs_ss, rs_rs)

    bv_out[0] = from_heads(branch_all, 0, br_ss, br_rs)
    bk_out[0] = from_heads(branch_all, 1, br_ss, br_rs)

    for at, (buf, into, ss, rs, out) in enumerate((
        (dq_send, dq_recv, dq_ss, dq_rs, dq_out), (att_send, att_recv, at_ss, at_rs, att_out)
    )):
        term = buf[mine, :].astype(F32)
        for d in range(1, n):
            remote(
                into.at[d - 1], into.at[d - 1], ss.at[d - 1], rs.at[d - 1], seq_to(d)
            ).wait_recv()
            term = term + into[d - 1].astype(F32)
        rows_f32[at] = term
        for i in range(answers):
            out[0, i] = rows_f32[at, i * per:(i + 1) * per, :].astype(out.dtype)

    rv_out[...] = from_heads(root_all, 0, rs_ss, rs_rs)
    rk_out[...] = from_heads(root_all, 1, rs_ss, rs_rs)

    for copy in sends:
        copy.wait_send()


def hand_out(*refs):
    sems = refs[12]
    copies = [pltpu.make_async_copy(refs[i], refs[6 + i], sems.at[i]) for i in range(6)]
    for copy in copies:
        copy.start()
    for copy in copies:
        copy.wait()


def per_device(sizes, queries, output_cotangent, root_keys, root_values, branch_keys,
               branch_values, answer_positions):
    n, heads, branches = sizes
    answers, per, width = queries.shape[1:]
    own = answers * per
    padded = -(-n * own // ROWS) * ROWS
    chunks = padded // ROWS
    root_rows, branch_rows = root_keys.shape[0], branch_keys.shape[1]
    key_rows = root_rows + branch_rows
    vmem = pl.BlockSpec(memory_space=pltpu.VMEM)
    whole = pl.BlockSpec(memory_space=pltpu.HBM)

    def sem(*shape):
        return pltpu.SemaphoreType.DMA(tuple(max(1, size) for size in shape))

    z, h, b = max(1, n - 1), max(1, heads - 1), max(1, branches - 1)
    scratch = [
        pltpu.VMEM(answer_positions.shape, jnp.int32),
        pltpu.VMEM((key_rows, width), BF16),
        pltpu.VMEM((key_rows, width), BF16),
        pltpu.VMEM((width, key_rows), BF16),
        pltpu.VMEM((width, key_rows), BF16),
        pltpu.VMEM((2, own, width), F32),
        pltpu.VMEM((padded, width), BF16),
        pltpu.VMEM((padded, width), BF16),
        pltpu.VMEM((n, chunks, 8, ROWS), F32),
        pltpu.VMEM((chunks, key_rows, ROWS), F32),
        pltpu.VMEM((chunks, key_rows, ROWS), F32),
        pltpu.VMEM((chunks, width, ROWS), F32),
        pltpu.VMEM((chunks, 8, ROWS), F32),
        pltpu.VMEM((padded, width), BF16),
        pltpu.VMEM((z, own, width), BF16),
        pltpu.VMEM((padded, width), BF16),
        pltpu.VMEM((z, own, width), BF16),
        pltpu.VMEM((b, padded, width), BF16),
        pltpu.VMEM((b, padded, width), BF16),
        pltpu.VMEM((b, chunks, root_rows, ROWS), F32),
        pltpu.VMEM((b, chunks, 8, ROWS), F32),
        pltpu.VMEM((2, branches, root_rows, width), F32),
        pltpu.VMEM((2, heads, root_rows, width), BF16),
        pltpu.VMEM((2, heads, branch_rows, width), BF16),
        pltpu.VMEM((chunks, key_rows, ROWS), BF16),
        pltpu.VMEM((branch_rows, width), F32),
        sem(7),
        sem(z), sem(z), sem(z), sem(z), sem(z), sem(z), sem(z), sem(z), sem(z), sem(z),
        sem(2, h), sem(2, h), sem(b), sem(b),
        sem(b, n), sem(b, n), sem(b, n), sem(b, n), sem(2, h), sem(2, h),
    ]
    outs = (
        jax.ShapeDtypeStruct(queries.shape, BF16),
        jax.ShapeDtypeStruct(queries.shape, F32),
        jax.ShapeDtypeStruct(root_keys.shape, F32),
        jax.ShapeDtypeStruct(root_values.shape, F32),
        jax.ShapeDtypeStruct(branch_keys.shape, F32),
        jax.ShapeDtypeStruct(branch_values.shape, F32),
    )
    results = pl.pallas_call(
        functools.partial(kernel, sizes),
        out_shape=outs,
        in_specs=[whole] * 7,
        out_specs=[vmem] * 6,
        scratch_shapes=scratch,
        compiler_params=pltpu.CompilerParams(
            collective_id=0, has_side_effects=True, vmem_limit_bytes=48 * 1024 * 1024
        ),
    )(*(
        pltpu.with_memory_space_constraint(array, pltpu.HBM) for array in (
            queries.reshape(own, width), output_cotangent.reshape(own, width),
            answer_positions, root_keys, root_values,
            branch_keys, branch_values,
        )
    ))
    return pl.pallas_call(
        hand_out,
        out_shape=outs,
        in_specs=[vmem] * 6,
        out_specs=[whole] * 6,
        scratch_shapes=[pltpu.SemaphoreType.DMA((6,))],
        compiler_params=pltpu.CompilerParams(vmem_limit_bytes=2 * 1024 * 1024),
    )(*results)


def solution(mesh):
    sizes = (mesh.shape["seq"], mesh.shape["head"], mesh.shape["branch"])
    rows = P(("parts", "branch"), "seq", "head", None)
    root = P(("parts", "seq"), None)
    branch = P(("parts", "branch"), "seq", None)
    return jax.shard_map(
        functools.partial(per_device, sizes),
        mesh=mesh,
        in_specs=(rows, rows, root, root, branch, branch, P(("parts", "branch"), None)),
        out_specs=(rows, rows, root, root, branch, branch),
        check_vma=False,
    )
```

```python
import functools
import math

import jax
import jax.numpy as jnp
from jax import lax
from jax.experimental import pallas as pl
from jax.experimental.pallas import tpu as pltpu
from jax.sharding import PartitionSpec as P

NEG = -1e30
ROWS = 256
F32 = jnp.float32
BF16 = jnp.bfloat16


def dot_last(left, right):
    return lax.dot_general(left, right, (((1,), (1,)), ((), ())), preferred_element_type=F32)


def dot_plain(left, right):
    return jnp.dot(left, right, preferred_element_type=F32)


def remote(src, dst, send, recv, device):
    return pltpu.make_async_remote_copy(
        src_ref=src,
        dst_ref=dst,
        send_sem=send,
        recv_sem=recv,
        device_id=device,
        device_id_type=pl.DeviceIdType.MESH,
    )


def over(count, body):
    if count == 1:
        body(0)
    else:
        lax.fori_loop(0, count, lambda at, carry: (body(at), carry)[1], 0)


def kernel(
    sizes,
    q_hbm, g_hbm, pos_hbm, rk_hbm, rv_hbm, bk_hbm, bv_hbm,
    att_out, dq_out, rk_out, rv_out, bk_out, bv_out,
    pos_ref, keys, values, keys_t, values_t, rows_f32, qbuf, gbuf, stats, probs, product, weighted, place,
    att_send, att_recv, dq_send, dq_recv,
    q_far, g_far, score_far, place_far, terms, root_all, branch_all, slope, grads,
    load_sem, q_ss, q_rs, g_ss, g_rs, st_ss, st_rs, at_ss, at_rs, dq_ss, dq_rs,
    rs_ss, rs_rs, x_ss, x_rs, xq_ss, xq_rs, xg_ss, xg_rs, br_ss, br_rs,
):
    n, heads, branches = sizes
    me, my_head, my_branch = (
        lax.axis_index("seq"), lax.axis_index("head"), lax.axis_index("branch")
    )
    own, width = q_hbm.shape
    answers, per = att_out.shape[1:3]
    padded = qbuf.shape[0]
    chunks = padded // ROWS
    root_rows, branch_rows = rk_hbm.shape[0], bk_hbm.shape[1]
    scale = 1.0 / math.sqrt(width)

    def seq_to(d):
        return {"seq": lax.rem(me + d, n)}

    def seq_from(d):
        return lax.rem(me - d + n, n)

    def head_to(d):
        return {"head": lax.rem(my_head + d, heads)}

    def head_from(d):
        return lax.rem(my_head - d + heads, heads)

    def branch_to(d):
        return {"branch": lax.rem(my_branch + d, branches)}

    def branch_from(d):
        return lax.rem(my_branch - d + branches, branches)

    barrier = pltpu.get_barrier_semaphore()
    for to, count in ((seq_to, n), (head_to, heads), (branch_to, branches)):
        for d in range(1, count):
            pl.semaphore_signal(
                barrier, inc=1, device_id=to(d), device_id_type=pl.DeviceIdType.MESH
            )

    mine = pl.ds(pl.multiple_of(me * own, 16), own)
    loads = [
        pltpu.make_async_copy(q_hbm, qbuf.at[mine], load_sem.at[4]),
        pltpu.make_async_copy(g_hbm, gbuf.at[mine], load_sem.at[5]),
        pltpu.make_async_copy(pos_hbm, pos_ref, load_sem.at[6]),
        pltpu.make_async_copy(rk_hbm, keys.at[pl.ds(0, root_rows)], load_sem.at[0]),
        pltpu.make_async_copy(bk_hbm.at[0], keys.at[pl.ds(root_rows, branch_rows)], load_sem.at[1]),
        pltpu.make_async_copy(rv_hbm, values.at[pl.ds(0, root_rows)], load_sem.at[2]),
        pltpu.make_async_copy(bv_hbm.at[0], values.at[pl.ds(root_rows, branch_rows)], load_sem.at[3]),
    ]
    for load in loads:
        load.start()

    pl.semaphore_wait(barrier, (n - 1) + (heads - 1) + (branches - 1))

    sends = []

    def send(*pieces):
        copy = remote(*pieces)
        copy.start()
        sends.append(copy)

    for source, buf, ss, rs in ((q_hbm, qbuf, q_ss, q_rs), (g_hbm, gbuf, g_ss, g_rs)):
        for d in range(1, n):
            send(source, buf.at[mine], ss.at[d - 1], rs.at[d - 1], seq_to(d))

    def across(buf, far, ss, rs, d):
        rows = pl.ds(pl.multiple_of(seq_from(d) * own, 16), own)
        source = buf if d == 0 else buf.at[rows]
        for e in range(1, branches):
            send(source, far.at[e - 1, rows], ss.at[e - 1, d], rs.at[e - 1, d], branch_to(e))

    across(q_hbm, q_far, xq_ss, xq_rs, 0)
    across(g_hbm, g_far, xg_ss, xg_rs, 0)

    if padded > n * own:
        for target in (qbuf, gbuf):
            target[n * own:, :] = jnp.zeros((padded - n * own, width), BF16)
        for target in (q_far, g_far):
            for e in range(1, branches):
                target[e - 1, n * own:, :] = jnp.zeros((padded - n * own, width), BF16)

    def arrived_rows(buf, ss, rs, far, far_ss, far_rs):
        for d in range(1, n):
            rows = pl.ds(pl.multiple_of(seq_from(d) * own, 16), own)
            remote(buf.at[rows], buf.at[rows], ss.at[d - 1], rs.at[d - 1], seq_to(d)).wait_recv()
            across(buf, far, far_ss, far_rs, d)

    loads[2].wait()
    total = pos_ref.shape[1]
    spot = jnp.broadcast_to(pos_ref[...], (8, total))
    high = (spot >> 7).astype(F32).astype(BF16)
    low = (spot & 127).astype(F32).astype(BF16)

    def expand(c):
        row = lax.broadcasted_iota(jnp.int32, (total, ROWS), 1) + c * ROWS
        answer = lax.broadcasted_iota(jnp.int32, (total, ROWS), 0)
        pick = (row >= answer * per) & (row < answer * per + per)
        pick = jnp.where(pick, 1.0, 0.0).astype(BF16)
        place[c] = dot_plain(high, pick) * 128.0 + dot_plain(low, pick)

    over(chunks, expand)

    for load in loads[:2] + loads[3:]:
        load.wait()
    values_t[...] = values[...].astype(F32).T.astype(BF16)
    arrived_rows(qbuf, q_ss, q_rs, q_far, xq_ss, xq_rs)

    key_place = (
        lax.broadcasted_iota(jnp.int32, (branch_rows, ROWS), 0) + me * branch_rows
    ).astype(F32)

    def rows_of(c):
        return pl.ds(c * ROWS if isinstance(c, int) else pl.multiple_of(c * ROWS, ROWS), ROWS)

    half = ROWS // 2

    def note(c, kind, row):
        stats[me, c, 2 * kind:2 * kind + 1, :] = row[:, :half]
        stats[me, c, 2 * kind + 1:2 * kind + 2, :] = row[:, half:]

    def noted(s, c, kind):
        first, last = 2 * kind, 2 * kind + 1
        return jnp.concatenate(
            [stats[s, c, first:first + 1, :], stats[s, c, last:last + 1, :]], axis=1
        )

    def scores(c):
        q = qbuf[rows_of(c), :]
        on_root = dot_last(keys[:root_rows, :], q) * scale
        on_branch = dot_last(keys[root_rows:, :], q) * scale
        on_branch = jnp.where(key_place <= place[c, 0:1, :], on_branch, NEG)
        peak = jnp.maximum(
            jnp.max(on_root, axis=0, keepdims=True), jnp.max(on_branch, axis=0, keepdims=True)
        )
        p_root = jnp.exp(on_root - peak)
        p_branch = jnp.exp(on_branch - peak)
        probs[c, :root_rows, :] = on_root
        probs[c, root_rows:, :] = p_branch
        sums = jnp.sum(p_root, axis=0, keepdims=True) + jnp.sum(p_branch, axis=0, keepdims=True)
        slope[c, :root_rows, :] = p_root.astype(BF16)
        slope[c, root_rows:, :] = p_branch.astype(BF16)
        note(c, 0, peak)
        note(c, 1, sums)

    over(chunks, scores)
    arrived_rows(gbuf, g_ss, g_rs, g_far, xg_ss, xg_rs)

    def dots(c):
        turned = gbuf[rows_of(c), :].astype(F32).T
        share = dot_plain(values_t[...], slope[c])
        weighted[c] = share
        note(c, 2, jnp.sum(share * turned, axis=0, keepdims=True))
        stats[me, c, 6:8, :] = jnp.zeros((2, half), F32)

    over(chunks, dots)
    for d in range(1, n):
        send(stats.at[me], stats.at[me], st_ss.at[d - 1], st_rs.at[d - 1], seq_to(d))

    def products(c):
        g = gbuf[rows_of(c), :]
        product[c, :root_rows, :] = dot_last(values[:root_rows, :], g)
        product[c, root_rows:, :] = dot_last(values[root_rows:, :], g)

    over(chunks, products)
    keys_t[...] = keys[...].astype(F32).T.astype(BF16)

    def arrived_far(far, ss, rs):
        for e in range(1, branches):
            for d in range(n):
                rows = far.at[e - 1, pl.ds(pl.multiple_of(seq_from(d) * own, 16), own)]
                remote(rows, rows, ss.at[e - 1, d], rs.at[e - 1, d], branch_to(e)).wait_recv()

    arrived_far(q_far, xq_ss, xq_rs)
    for e in range(1, branches):

        def far_scores(c, e=e):
            q = q_far[e - 1, rows_of(c), :]
            score_far[e - 1, c] = dot_last(keys[:root_rows, :], q) * scale

        over(chunks, far_scores)

    for d in range(1, n):
        at = seq_from(d)
        remote(stats.at[at], stats.at[at], st_ss.at[d - 1], st_rs.at[d - 1], seq_to(d)).wait_recv()

    def combine(c):
        peak = noted(0, c, 0)
        for s in range(1, n):
            peak = jnp.maximum(peak, noted(s, c, 0))
        sums, dotted = jnp.zeros((1, ROWS), F32), jnp.zeros((1, ROWS), F32)
        for s in range(n):
            factor = jnp.exp(noted(s, c, 0) - peak)
            sums = sums + noted(s, c, 1) * factor
            dotted = dotted + noted(s, c, 2) * factor
        factor = jnp.exp(noted(me, c, 0) - peak) / sums
        place[c, 1:2, :] = factor
        place[c, 2:3, :] = dotted / sums
        place[c, 3:4, :] = peak
        place[c, 4:5, :] = 1.0 / sums

    over(chunks, combine)

    for e in range(1, branches):
        send(place, place_far.at[e - 1], x_ss.at[e - 1], x_rs.at[e - 1], branch_to(e))

    def share_rows(buf, into, ss, rs):
        for d in range(1, n):
            far = pl.ds(pl.multiple_of(lax.rem(me + d, n) * own, 16), own)
            send(buf.at[far], into.at[d - 1], ss.at[d - 1], rs.at[d - 1], seq_to(d))

    def shares(c):
        att_send[rows_of(c), :] = (weighted[c] * place[c, 1:2, :]).T.astype(BF16)

    over(chunks, shares)
    share_rows(att_send, att_recv, at_ss, at_rs)

    def root_weights(score, norm):
        return jnp.exp(score - norm[3:4, :]) * norm[4:5, :]

    def root_value_term(score, norm, g):
        return dot_plain(root_weights(score, norm).astype(BF16), g)

    def root_key_term(score, gap, norm, q):
        sloped = (root_weights(score, norm) * (gap - norm[2:3, :])).astype(BF16)
        return sloped, dot_plain(sloped, q) * scale

    def put(at, branch, c, term):
        if chunks == 1:
            terms[at, branch] = term
            return
        kept = jnp.where(c == 0, 0.0, terms[at, branch])
        terms[at, branch] = kept + term

    def own_root_keys(c):
        score, gap = probs[c, :root_rows, :], product[c, :root_rows, :]
        sloped, term = root_key_term(score, gap, place[c], qbuf[rows_of(c), :])
        slope[c, :root_rows, :] = sloped
        put(1, my_branch, c, term)

    def own_root_values(c):
        score, norm = probs[c, :root_rows, :], place[c]
        put(0, my_branch, c, root_value_term(score, norm, gbuf[rows_of(c), :]))

    def branch_value_term(c):
        weights = probs[c, root_rows:, :] * place[c, 1:2, :]
        return dot_plain(weights.astype(BF16), gbuf[rows_of(c), :])

    def branch_key_term(c):
        weights = probs[c, root_rows:, :] * place[c, 1:2, :]
        gap = product[c, root_rows:, :] - place[c, 2:3, :]
        sloped = (weights * gap).astype(BF16)
        slope[c, root_rows:, :] = sloped
        return dot_plain(sloped, qbuf[rows_of(c), :]) * scale

    def sweep(term, count):
        if chunks == 1:
            return term(0)
        grads[:count, :] = jnp.zeros((count, width), F32)

        def add(c):
            grads[:count, :] += term(c)

        over(chunks, add)
        return grads[:count, :]

    def to_heads(buf, at, term, ss, rs):
        buf[at, my_head] = term.astype(BF16)
        block = buf.at[at, my_head]
        for d in range(1, heads):
            send(block, block, ss.at[at, d - 1], rs.at[at, d - 1], head_to(d))

    def from_heads(buf, at, ss, rs):
        for d in range(1, heads):
            block = buf.at[at, head_from(d)]
            remote(block, block, ss.at[at, d - 1], rs.at[at, d - 1], head_to(d)).wait_recv()
        term = buf[at, 0].astype(F32)
        for h in range(1, heads):
            term = term + buf[at, h].astype(F32)
        return term

    def query_terms(c):
        term = dot_plain(keys_t[...], slope[c]) * scale
        dq_send[rows_of(c), :] = term.T.astype(BF16)

    over(chunks, own_root_keys)
    to_heads(branch_all, 1, sweep(branch_key_term, branch_rows), br_ss, br_rs)
    over(chunks, query_terms)
    share_rows(dq_send, dq_recv, dq_ss, dq_rs)
    to_heads(branch_all, 0, sweep(branch_value_term, branch_rows), br_ss, br_rs)
    over(chunks, own_root_values)

    arrived_far(g_far, xg_ss, xg_rs)
    for e in range(1, branches):
        norms = place_far.at[e - 1]
        remote(norms, norms, x_ss.at[e - 1], x_rs.at[e - 1], branch_to(e)).wait_recv()

    def far_values(e, c):
        term = root_value_term(score_far[e - 1, c], place_far[e - 1, c], g_far[e - 1, rows_of(c), :])
        put(0, branch_from(e), c, term)

    def far_keys(e, c):
        gap = dot_last(values[:root_rows, :], g_far[e - 1, rows_of(c), :])
        q = q_far[e - 1, rows_of(c), :]
        put(1, branch_from(e), c, root_key_term(score_far[e - 1, c], gap, place_far[e - 1, c], q)[1])

    for at, far in enumerate((far_values, far_keys)):
        for e in range(1, branches):
            over(chunks, functools.partial(far, e))
        term = terms[at, 0]
        for b in range(1, branches):
            term = term + terms[at, b]
        to_heads(root_all, at, term, rs_ss, rs_rs)

    bv_out[0] = from_heads(branch_all, 0, br_ss, br_rs)
    bk_out[0] = from_heads(branch_all, 1, br_ss, br_rs)

    for at, (buf, into, ss, rs, out) in enumerate((
        (dq_send, dq_recv, dq_ss, dq_rs, dq_out), (att_send, att_recv, at_ss, at_rs, att_out)
    )):
        term = buf[mine, :].astype(F32)
        for d in range(1, n):
            remote(
                into.at[d - 1], into.at[d - 1], ss.at[d - 1], rs.at[d - 1], seq_to(d)
            ).wait_recv()
            term = term + into[d - 1].astype(F32)
        rows_f32[at] = term
        for i in range(answers):
            out[0, i] = rows_f32[at, i * per:(i + 1) * per, :].astype(out.dtype)

    rv_out[...] = from_heads(root_all, 0, rs_ss, rs_rs)
    rk_out[...] = from_heads(root_all, 1, rs_ss, rs_rs)

    for copy in sends:
        copy.wait_send()


def hand_out(*refs):
    sems = refs[12]
    copies = [pltpu.make_async_copy(refs[i], refs[6 + i], sems.at[i]) for i in range(6)]
    for copy in copies:
        copy.start()
    for copy in copies:
        copy.wait()


def per_device(sizes, queries, output_cotangent, root_keys, root_values, branch_keys,
               branch_values, answer_positions):
    n, heads, branches = sizes
    answers, per, width = queries.shape[1:]
    own = answers * per
    padded = -(-n * own // ROWS) * ROWS
    chunks = padded // ROWS
    root_rows, branch_rows = root_keys.shape[0], branch_keys.shape[1]
    key_rows = root_rows + branch_rows
    vmem = pl.BlockSpec(memory_space=pltpu.VMEM)
    whole = pl.BlockSpec(memory_space=pltpu.HBM)

    def sem(*shape):
        return pltpu.SemaphoreType.DMA(tuple(max(1, size) for size in shape))

    z, h, b = max(1, n - 1), max(1, heads - 1), max(1, branches - 1)
    scratch = [
        pltpu.VMEM(answer_positions.shape, jnp.int32),
        pltpu.VMEM((key_rows, width), BF16),
        pltpu.VMEM((key_rows, width), BF16),
        pltpu.VMEM((width, key_rows), BF16),
        pltpu.VMEM((width, key_rows), BF16),
        pltpu.VMEM((2, own, width), F32),
        pltpu.VMEM((padded, width), BF16),
        pltpu.VMEM((padded, width), BF16),
        pltpu.VMEM((n, chunks, 8, ROWS // 2), F32),
        pltpu.VMEM((chunks, key_rows, ROWS), F32),
        pltpu.VMEM((chunks, key_rows, ROWS), F32),
        pltpu.VMEM((chunks, width, ROWS), F32),
        pltpu.VMEM((chunks, 8, ROWS), F32),
        pltpu.VMEM((padded, width), BF16),
        pltpu.VMEM((z, own, width), BF16),
        pltpu.VMEM((padded, width), BF16),
        pltpu.VMEM((z, own, width), BF16),
        pltpu.VMEM((b, padded, width), BF16),
        pltpu.VMEM((b, padded, width), BF16),
        pltpu.VMEM((b, chunks, root_rows, ROWS), F32),
        pltpu.VMEM((b, chunks, 8, ROWS), F32),
        pltpu.VMEM((2, branches, root_rows, width), F32),
        pltpu.VMEM((2, heads, root_rows, width), BF16),
        pltpu.VMEM((2, heads, branch_rows, width), BF16),
        pltpu.VMEM((chunks, key_rows, ROWS), BF16),
        pltpu.VMEM((branch_rows, width), F32),
        sem(7),
        sem(z), sem(z), sem(z), sem(z), sem(z), sem(z), sem(z), sem(z), sem(z), sem(z),
        sem(2, h), sem(2, h), sem(b), sem(b),
        sem(b, n), sem(b, n), sem(b, n), sem(b, n), sem(2, h), sem(2, h),
    ]
    outs = (
        jax.ShapeDtypeStruct(queries.shape, BF16),
        jax.ShapeDtypeStruct(queries.shape, F32),
        jax.ShapeDtypeStruct(root_keys.shape, F32),
        jax.ShapeDtypeStruct(root_values.shape, F32),
        jax.ShapeDtypeStruct(branch_keys.shape, F32),
        jax.ShapeDtypeStruct(branch_values.shape, F32),
    )
    results = pl.pallas_call(
        functools.partial(kernel, sizes),
        out_shape=outs,
        in_specs=[whole] * 7,
        out_specs=[vmem] * 6,
        scratch_shapes=scratch,
        compiler_params=pltpu.CompilerParams(
            collective_id=0, has_side_effects=True, vmem_limit_bytes=48 * 1024 * 1024
        ),
    )(*(
        pltpu.with_memory_space_constraint(array, pltpu.HBM) for array in (
            queries.reshape(own, width), output_cotangent.reshape(own, width),
            answer_positions, root_keys, root_values,
            branch_keys, branch_values,
        )
    ))
    return pl.pallas_call(
        hand_out,
        out_shape=outs,
        in_specs=[vmem] * 6,
        out_specs=[whole] * 6,
        scratch_shapes=[pltpu.SemaphoreType.DMA((6,))],
        compiler_params=pltpu.CompilerParams(vmem_limit_bytes=2 * 1024 * 1024),
    )(*results)


def solution(mesh):
    sizes = (mesh.shape["seq"], mesh.shape["head"], mesh.shape["branch"])
    rows = P(("parts", "branch"), "seq", "head", None)
    root = P(("parts", "seq"), None)
    branch = P(("parts", "branch"), "seq", None)
    return jax.shard_map(
        functools.partial(per_device, sizes),
        mesh=mesh,
        in_specs=(rows, rows, root, root, branch, branch, P(("parts", "branch"), None)),
        out_specs=(rows, rows, root, root, branch, branch),
        check_vma=False,
    )
```
